32 devices in a mesh: ctx: 8 (over y, x, core), hx: 4 (over z).
Axes of the slice: x: 2, y: 2, z: 4, core: 2. Of those that a mesh axis runs over, the one named last changes fastest.
Arguments:
- tokens: bfloat16 [4096, 5120], P('ctx'), may hold values from -6 to 6
- attn_gain: bfloat16 [5120], replicated, may hold values from 0.5 to 1.5
- ffn_gain: bfloat16 [5120], replicated, may hold values from 0.5 to 1.5
- w_query: bfloat16 [5120, 3072], P('ctx', 'hx'), may hold values from -3 to 3
- w_key: bfloat16 [5120, 1024], P('ctx', 'hx'), may hold values from -1 to 1
- w_value: bfloat16 [5120, 1024], P('ctx', 'hx'), may hold values from -0.078125 to 0.078125
- w_out: bfloat16 [3072, 5120], P('hx'), may hold values from -0.109375 to 0.109375
- w_router: bfloat16 [5120, 8], replicated, may hold values from -0.078125 to 0.078125
- routes: int32 [4096, 1], P('ctx'), may hold values from 0 to 7; in each aligned block of 512 rows (0 to 511, 512 to 1023, ...) at most 64 rows name the same one
- w_gate: bfloat16 [8, 5120, 4096], P('ctx', None, 'hx'), may hold values from -0.078125 to 0.078125
- w_up: bfloat16 [8, 5120, 4096], P('ctx', None, 'hx'), may hold values from -0.078125 to 0.078125
- w_down: bfloat16 [8, 4096, 5120], P('ctx', 'hx'), may hold values from -0.09375 to 0.09375
Outputs:
- layer_out: bfloat16 [4096, 5120], P('ctx', 'hx')
The draws below stay inside these ranges and needn't reach their ends.
Inputs may be any that keep to these rules, and one draw needn't show every extreme that they name: `routes`: within the 512 rows of one device, no expert is named by more than 64 rows, a bound that some block reaches.
All inputs are finite; a program needn't handle non-finite values.
Results may differ from the reference program's by a relative error of at most 0.0095.
Values may be sent and summed in bfloat16 or wider, within the bound.
No kernel may reach another device: no remote copies, remote signals or barrier semaphores. Data moves between devices by JAX's collectives and lax.ppermute only.
A program may use at most 128 MiB of HBM per device.

```python
import math
import jax
import jax.numpy as jnp
import numpy as np
from jax import lax

D = 5120
HEADS = 24
KV_HEADS = 8
HD = 128
FF = 4096
TOK_DEV = 512
TOKENS = 4096
EXPERTS = 8
CAP = 64
N_CTX = 8
N_HX = 4


def draw_tokens(key, part):
    normal_values = jax.random.normal(jax.random.fold_in(key, 21), (TOKENS, D), jnp.float32)
    return jnp.clip(normal_values, -6.0, 6.0).astype(jnp.bfloat16)


def attention_weights(key):
    key_mat = jax.random.normal(jax.random.fold_in(key, 11), (D, KV_HEADS, HD), jnp.float32) * D ** (-0.5)
    loose = jax.random.normal(jax.random.fold_in(key, 12), (D, HEADS, HD), jnp.float32) * D ** (-0.5)
    return (key_mat.reshape(D, KV_HEADS * HD), loose.reshape(D, HEADS * HD))


def draw_w_query(key, part):
    key_mat, loose = attention_weights(key)
    return jnp.clip(loose, -3.0, 3.0).astype(jnp.bfloat16)


def draw_w_key(key, part):
    key_mat, loose = attention_weights(key)
    return jnp.clip(key_mat, -1.0, 1.0).astype(jnp.bfloat16)


def steps_of(stream_key, dims, pieces, smallest, top_value):
    def one(dim, shards_of):
        steps = jax.random.uniform(jax.random.fold_in(jax.random.fold_in(stream_key, 6), dim), (shards_of,), jnp.float32, smallest / len(pieces), top_value / len(pieces))
        return jnp.repeat(jnp.exp(steps), dims[dim] // shards_of).reshape((-1,) + (1,) * (len(dims) - dim - 1))

    factor_of = one(*pieces[0])
    for cut in pieces[1:]:
        factor_of = factor_of * one(*cut)
    return factor_of


def shared_out(key, own, number, rows, amount, top, reach, lean):
    order = jax.random.permutation(key, amount)
    heavy_load, ordinary = portions_of(amount, rows * top, reach, lean, True), portions_of(amount, rows * top, reach, lean, False)
    places = jnp.arange(amount)

    def named(tallies, turn):
        used = int((tallies > 0).sum())
        fixed = max(1, used // 4)
        moved = fixed + (places - fixed + turn * (used - fixed)) % max(1, amount - fixed)
        return jnp.zeros((amount,), jnp.int32).at[order[jnp.where(places < fixed, places, moved)]].set(jnp.asarray(tallies, jnp.int32))

    tallies = jnp.where(number % 4 == 0, named(heavy_load, number // 4), named(ordinary, number - number // 4 - 1))
    mixed = jax.random.permutation(jax.random.fold_in(own, 3), amount)
    giver, taker = mixed[0:amount // 2 * 2:2], mixed[1:amount // 2 * 2:2]
    margin = jnp.minimum(tallies[giver] - 1, reach - tallies[taker]) // 2
    margin = jnp.where((giver == order[0]) | (taker == order[0]) | (tallies[taker] == 0), 0, jnp.maximum(margin, 0))
    moved = jax.random.randint(jax.random.fold_in(own, 4), (amount // 2,), 0, 1 << 20) % (margin + 1)
    tallies = tallies.at[giver].add(-moved).at[taker].add(moved)
    labels = jnp.searchsorted(jnp.cumsum(tallies), jnp.arange(rows * top), side="right").astype(jnp.int32)
    listing = labels.reshape(top, rows).T
    listing = listing[jax.random.permutation(jax.random.fold_in(own, 1), rows)]
    turn = jax.random.randint(jax.random.fold_in(own, 2), (rows, 1), 0, top)
    return jnp.take_along_axis(listing, (jnp.arange(top)[None, :] + turn) % top, axis=1)


def portions_of(amount, total, bound, skew, full):
    loads = [(1 << 20) // math.isqrt(rank ** skew) + 1 for rank in range(1, amount + 1)]
    largest = bound if full else min(bound, max(-(-total // amount), total * loads[0] // sum(loads)))
    least = 1 if total - largest >= amount - 1 else 0
    given, rest = [largest] + [least] * (amount - 1), total - largest - least * (amount - 1)
    while rest > 0:
        movable = [i for i in range(1, amount) if given[i] < largest] or [i for i in range(1, amount) if given[i] < bound]
        whole, remaining = sum([loads[i] for i in movable]), rest
        for i in movable:
            addition = min(bound - given[i], max(1, remaining * loads[i] // whole), rest)
            given[i] = given[i] + addition
            rest = rest - addition
    return np.array(given)


def bell_draw(key, extent, scale, bound, cuts=(), held_as=jnp.bfloat16):
    values = jax.random.normal(key, extent, jnp.float32) * scale
    if len(cuts) > 0:
        values = steps_of(key, extent, cuts, -0.22, 0.18) * values
    return jnp.clip(values, min=-bound, max=bound).astype(held_as)


def setup_inputs(seed: int = 0) -> dict:
    streams_of = jax.random.split(jax.random.key(seed), 13)
    tokens = draw_tokens(jax.random.fold_in(streams_of[12], 71), 0)
    attn_gain = jnp.clip(1.0 + 0.1 * jax.random.normal(streams_of[1], (D,), jnp.float32), 0.5, 1.5).astype(jnp.bfloat16)
    ffn_gain = jnp.clip(1.0 + 0.1 * jax.random.normal(streams_of[2], (D,), jnp.float32), 0.5, 1.5).astype(jnp.bfloat16)
    w_query = draw_w_query(jax.random.fold_in(streams_of[12], 71), 0)
    w_key = draw_w_key(jax.random.fold_in(streams_of[12], 71), 0)
    w_value = bell_draw(streams_of[5], (D, KV_HEADS * HD), D ** -0.5, 0.078125, ((0, 8), (1, 4)))
    w_out = bell_draw(streams_of[6], (HEADS * HD, D), (HEADS * HD) ** -0.5, 0.109375, ((0, 4),))
    w_router = bell_draw(streams_of[7], (D, EXPERTS), D ** -0.5, 0.078125)
    routes_keys = jax.random.split(jax.random.fold_in(streams_of[8], 1), TOKENS // TOK_DEV)
    routes_turns = jax.random.permutation(jax.random.fold_in(streams_of[8], 3), TOKENS // TOK_DEV)
    routes = jax.vmap(lambda own, number: shared_out(jax.random.fold_in(streams_of[8], 2), own, number, TOK_DEV, EXPERTS, 1, CAP, 2))(routes_keys, routes_turns).reshape((TOKENS, 1))
    w_gate = bell_draw(streams_of[9], (EXPERTS, D, FF), D ** -0.5, 0.078125, ((0, 8), (2, 4)))
    w_up = bell_draw(streams_of[10], (EXPERTS, D, FF), D ** -0.5, 0.078125, ((0, 8), (2, 4)))
    w_down = bell_draw(streams_of[11], (EXPERTS, FF, D), FF ** -0.5, 0.09375, ((0, 8), (1, 4)))
    return dict(tokens=tokens, attn_gain=attn_gain, ffn_gain=ffn_gain, w_query=w_query, w_key=w_key, w_value=w_value, w_out=w_out, w_router=w_router, routes=routes, w_gate=w_gate, w_up=w_up, w_down=w_down)


epsilon = 1e-05

def root_norm(values, gains):
    floats = values.astype(jnp.float32)
    inverse = lax.rsqrt(lax.optimization_barrier(jnp.mean(floats * floats, axis=-1, keepdims=True)) + epsilon)
    return (floats * inverse * gains.astype(jnp.float32)).astype(jnp.bfloat16)

def reference(tokens, attn_gain, ffn_gain, w_query, w_key, w_value, w_out, w_router, routes, w_gate, w_up, w_down):
    normed = root_norm(tokens, attn_gain)
    queries = jnp.dot(normed, w_query, preferred_element_type=jnp.float32).astype(jnp.bfloat16)
    key_proj = jnp.dot(normed, w_key, preferred_element_type=jnp.float32).astype(jnp.bfloat16)
    value_proj = jnp.dot(normed, w_value, preferred_element_type=jnp.float32).astype(jnp.bfloat16)
    group_size = HEADS // KV_HEADS
    head_share = HEADS * HD // N_HX
    queries_all = queries.reshape(TOKENS, KV_HEADS, group_size, HD)
    key_heads = key_proj.reshape(TOKENS, KV_HEADS, HD).astype(jnp.float32)
    value_heads = value_proj.reshape(TOKENS, KV_HEADS, HD).astype(jnp.float32)
    key_pos = jnp.arange(TOKENS, dtype=jnp.int32)
    out_groups = w_out.reshape(N_HX, head_share, D).astype(jnp.float32)

    def attend(block_index):
        begin = block_index * TOK_DEV
        queries_block = lax.dynamic_slice_in_dim(queries_all, begin, TOK_DEV, 0).astype(jnp.float32)
        scores = jnp.einsum('tkgd,skd->tkgs', queries_block, key_heads) * HD ** (-0.5)
        query_pos = begin + jnp.arange(TOK_DEV, dtype=jnp.int32)
        visible = (key_pos[None, :] <= query_pos[:, None])[:, None, None, :]
        masked = jnp.where(visible, scores, -jnp.inf)
        row_max = lax.optimization_barrier(jnp.max(masked, axis=-1, keepdims=True))
        weights = jnp.where(visible, jnp.exp(scores - row_max), 0.0)
        weight_sum = lax.optimization_barrier(jnp.sum(weights, axis=-1))
        rounded = lax.optimization_barrier(weights.astype(jnp.bfloat16))
        mixed = jnp.einsum('tkgs,skd->tkgd', rounded.astype(jnp.float32), value_heads)
        attended = (mixed / weight_sum[..., None]).astype(jnp.bfloat16).reshape(TOK_DEV, N_HX, head_share)
        partial_out = jnp.einsum('tgh,ghd->tgd', attended.astype(jnp.float32), out_groups)
        rounded_out = lax.optimization_barrier(partial_out.astype(jnp.bfloat16))
        return lax.optimization_barrier(jnp.sum(rounded_out.astype(jnp.float32), axis=1))
    attn_sum = lax.map(attend, jnp.arange(N_CTX, dtype=jnp.int32)).reshape(TOKENS, D)
    stream = (tokens.astype(jnp.float32) + attn_sum).astype(jnp.bfloat16)
    normed2 = root_norm(stream, ffn_gain)
    logits = jnp.dot(normed2, w_router, preferred_element_type=jnp.float32)
    chosen = routes[:, 0].astype(jnp.int32)
    onehot = chosen[:, None] == jnp.arange(EXPERTS, dtype=jnp.int32)[None, :]
    router_score = jax.nn.sigmoid(lax.optimization_barrier(jnp.sum(jnp.where(onehot, logits, 0.0), axis=-1)))
    routed = (normed2.astype(jnp.float32) * router_score[:, None]).astype(jnp.bfloat16)
    counts = jnp.cumsum(onehot.astype(jnp.int32).reshape(N_CTX, TOK_DEV, EXPERTS), axis=1).reshape(TOKENS, EXPERTS)
    position = lax.optimization_barrier(jnp.sum(jnp.where(onehot, counts, 0), axis=-1)).astype(jnp.int32) - 1
    block_of = jnp.arange(TOKENS, dtype=jnp.int32) // TOK_DEV
    slot_index = (chosen * (N_CTX * CAP) + block_of * CAP + position).astype(jnp.int32)
    buffer = jnp.zeros((EXPERTS * N_CTX * CAP, D), jnp.bfloat16).at[slot_index].set(routed)
    buffer = buffer.reshape(EXPERTS, N_CTX * CAP, D)
    hidden_share = FF // N_HX

    def expert(operands):
        expert_rows, gate_mat, up_mat, down_mat = operands
        gate_out = jnp.dot(expert_rows, gate_mat, preferred_element_type=jnp.float32)
        up_out = jnp.dot(expert_rows, up_mat, preferred_element_type=jnp.float32)
        hidden = (jax.nn.silu(gate_out) * up_out).astype(jnp.bfloat16)
        parts = jnp.einsum('rgf,gfd->rgd', hidden.reshape(N_CTX * CAP, N_HX, hidden_share).astype(jnp.float32), down_mat.reshape(N_HX, hidden_share, D).astype(jnp.float32))
        rounded_parts = lax.optimization_barrier(parts.astype(jnp.bfloat16))
        return lax.optimization_barrier(jnp.sum(rounded_parts.astype(jnp.float32), axis=1)).astype(jnp.bfloat16)
    expert_all = lax.map(expert, (buffer, w_gate, w_up, w_down)).reshape(EXPERTS * N_CTX * CAP, D)
    expert_out = expert_all[slot_index]
    return (stream.astype(jnp.float32) + expert_out.astype(jnp.float32)).astype(jnp.bfloat16)
```

```python
import functools

import jax
import jax.numpy as jnp
from jax import lax
from jax.experimental import pallas as pl
from jax.experimental.pallas import tpu as pltpu
from jax.sharding import PartitionSpec as P

HD = 128
epsilon = 1e-05
LOG2E = 1.4426950408889634
CHUNKS = 2
F32 = jnp.float32
BF16 = jnp.bfloat16


def dot32(left, right):
    return jnp.dot(left, right, preferred_element_type=F32)


def root_norm(values, gains):
    floats = values.astype(F32)
    inverse = lax.rsqrt(jnp.mean(floats * floats, axis=-1, keepdims=True) + epsilon)
    return (floats * inverse * gains.astype(F32)).astype(BF16)


def swap(value, axis, offset):
    count = lax.axis_size(axis)
    return lax.ppermute(value, axis, [(i, i ^ offset) for i in range(count)])


def xor_gather(block):
    count = lax.axis_size("ctx")
    half = block.shape[0] // 2
    held = {0: block}
    for offset in sorted(range(2, count, 2), key=lambda o: (o.bit_count(), o)):
        low = offset & -offset
        high = 1 << (offset.bit_length() - 1)
        if low == high:
            held[offset] = swap(block, "ctx", offset)
        else:
            top = swap(held[offset ^ low][:half], "ctx", low)
            bottom = swap(held[offset ^ high][half:], "ctx", high)
            held[offset] = jnp.concatenate([top, bottom], axis=0)
    if count > 1:
        for offset in range(0, count, 2):
            held[offset ^ 1] = swap(held[offset], "ctx", 1)
    return held


def line_gather(block):
    count = lax.axis_size("hx")
    own = lax.axis_index("hx")
    right = left = block
    rights, lefts = [], []
    for step in range(1, count):
        right = lax.ppermute(right, "hx", [(i, i + 1) for i in range(step - 1, count - 1)])
        left = lax.ppermute(left, "hx", [(i + 1, i) for i in range(0, count - step)])
        rights.append(right)
        lefts.append(left)
    return [block] + [
        jnp.where(own >= k, rights[k - 1], lefts[count - k - 1]) for k in range(1, count)
    ]


def line_scatter(values):
    count = lax.axis_size("hx")
    own = lax.axis_index("hx")
    width = values.shape[1] // count

    def share(index):
        index = jnp.clip(index, 0, count - 1)
        return lax.dynamic_slice_in_dim(values, index * width, width, 1)

    right = left = None
    for step in range(1, count):
        to_right = share(count - step + own)
        to_left = share(own + step - count)
        if right is not None:
            to_right = (to_right.astype(F32) + right.astype(F32)).astype(BF16)
            to_left = (to_left.astype(F32) + left.astype(F32)).astype(BF16)
        right = lax.ppermute(to_right, "hx", [(i, i + 1) for i in range(step)])
        left = lax.ppermute(to_left, "hx", [(i, i - 1) for i in range(count - step, count)])
    total = share(own).astype(F32)
    if right is not None:
        total = total + right.astype(F32) + left.astype(F32)
    return total.astype(BF16)


def attend_kernel(index_ref, query_ref, key_ref, value_ref, out_ref, *, group_size):
    rows = query_ref.shape[0]
    own = index_ref[0]
    scale = HD ** (-0.5) * LOG2E
    queries = [query_ref[:, g * HD : (g + 1) * HD] for g in range(group_size)]

    def block(start, states, masked):
        keys = key_ref[pl.ds(start, rows), :]
        values = value_ref[pl.ds(start, rows), :]
        states_out = []
        for query, (top, total, acc) in zip(queries, states):
            scores = lax.dot_general(
                keys, query, (((1,), (1,)), ((), ())), preferred_element_type=F32
            )
            if masked:
                key_at = lax.broadcasted_iota(jnp.int32, scores.shape, 0)
                query_at = lax.broadcasted_iota(jnp.int32, scores.shape, 1)
                scores = jnp.where(key_at <= query_at, scores, -1e30)
            new_top = jnp.maximum(top, jnp.max(scores, axis=0, keepdims=True))
            weights = jnp.exp2((scores - new_top) * scale)
            factor = jnp.exp2((top - new_top) * scale)
            total = total * factor + jnp.sum(weights, axis=0, keepdims=True)
            mixed = lax.dot_general(
                values,
                weights.astype(BF16),
                (((0,), (0,)), ((), ())),
                preferred_element_type=F32,
            )
            states_out.append((new_top, total, acc * factor + mixed))
        return tuple(states_out)

    start_state = tuple(
        (
            jnp.full((1, rows), -1e30, F32),
            jnp.zeros((1, rows), F32),
            jnp.zeros((HD, rows), F32),
        )
        for _ in range(group_size)
    )
    states = block(pl.multiple_of(own * rows, rows), start_state, True)
    states = lax.fori_loop(
        0, own, lambda j, held: block(pl.multiple_of(j * rows, rows), held, False), states
    )
    for g, (_, total, acc) in enumerate(states):
        out_ref[:, g * HD : (g + 1) * HD] = (acc / total).T.astype(BF16)


def attend(own, queries, keys, values):
    rows, width = queries.shape
    group_size = width // HD
    return pl.pallas_call(
        functools.partial(attend_kernel, group_size=group_size),
        out_shape=jax.ShapeDtypeStruct((rows, width), BF16),
        grid_spec=pltpu.PrefetchScalarGridSpec(
            num_scalar_prefetch=1,
            grid=(1,),
            in_specs=[
                pl.BlockSpec(queries.shape, lambda g, s: (0, 0)),
                pl.BlockSpec(keys.shape, lambda g, s: (0, 0)),
                pl.BlockSpec(values.shape, lambda g, s: (0, 0)),
            ],
            out_specs=pl.BlockSpec((rows, width), lambda g, s: (0, 0)),
        ),
        compiler_params=pltpu.CompilerParams(vmem_limit_bytes=48 * 1024 * 1024),
        cost_estimate=pl.CostEstimate(
            flops=4 * rows * keys.shape[0] * width,
            bytes_accessed=4 * keys.size,
            transcendentals=rows * keys.shape[0] * group_size,
        ),
        name="attend",
    )(own, queries, keys, values)


def body(
    tokens,
    attn_gain,
    ffn_gain,
    w_query,
    w_key,
    w_value,
    w_out,
    w_router,
    routes,
    w_gate,
    w_up,
    w_down,
):
    ctx_count = lax.axis_size("ctx")
    hx_count = lax.axis_size("hx")
    ctx_index = lax.axis_index("ctx")
    hx_index = lax.axis_index("hx")
    parity = ctx_index % 2
    tok_rows, full_width = tokens.shape
    width = full_width // hx_count
    own_rows = w_query.shape[0]
    kv_heads = w_key.shape[1] // HD
    group_width = w_query.shape[1] // kv_heads
    expert_count = w_router.shape[1]

    half = width // 2
    out_mats = []
    for k in range(hx_count):
        dest = (hx_index + k) % hx_count
        mine = lax.dynamic_slice_in_dim(w_out, dest * width + parity * half, half, 1)
        if k > 0:
            mine = lax.ppermute(
                mine, "hx", [(i, (i + k) % hx_count) for i in range(hx_count)]
            )
            other = swap(mine, "ctx", 1)
        else:
            other = lax.dynamic_slice_in_dim(w_out, dest * width + (1 - parity) * half, half, 1)
        out_mats.append((mine, other))

    normed = root_norm(tokens, attn_gain)
    offsets = range(ctx_count)
    normed_at = [
        lax.dynamic_slice_in_dim(normed, (ctx_index ^ o) * own_rows, own_rows, 1) for o in offsets
    ]

    def project(blocks):
        total = dot32(normed_at[0], blocks[0])
        for o in offsets[1:]:
            total = total + dot32(normed_at[o], blocks[o])
        return total.astype(BF16)

    kv_own = project(xor_gather(jnp.concatenate([w_key, w_value], axis=1)))
    kv_blocks = xor_gather(kv_own)
    kv_all = jnp.zeros((ctx_count * tok_rows, kv_own.shape[1]), BF16)
    for o in offsets:
        kv_all = lax.dynamic_update_slice_in_dim(
            kv_all, kv_blocks[o], (ctx_index ^ o) * tok_rows, 0
        )

    attended = []
    for g in range(kv_heads):
        queries = project(xor_gather(w_query[:, g * group_width : (g + 1) * group_width]))
        mixed = attend(
            ctx_index.reshape(1),
            queries,
            kv_all[:, g * HD : (g + 1) * HD],
            kv_all[:, (kv_heads + g) * HD : (kv_heads + g + 1) * HD],
        )
        attended.append(line_gather(mixed))

    chosen = routes[:, 0]
    onehot = chosen[:, None] == jnp.arange(expert_count, dtype=jnp.int32)[None, :]
    counts = jnp.cumsum(onehot.astype(jnp.int32), axis=0)
    position = jnp.sum(jnp.where(onehot, counts, 0), axis=-1) - 1
    capacity = tok_rows // 8
    part = capacity // CHUNKS
    exp_local = w_gate.shape[0]
    slot_expert = jnp.arange(expert_count * part, dtype=jnp.int32) // part
    slot_place = jnp.arange(expert_count * part, dtype=jnp.int32) % part
    pickers = [
        (
            (slot_expert[:, None] == chosen[None, :])
            & (slot_place[:, None] + c * part == position[None, :])
        ).astype(BF16)
        for c in range(CHUNKS)
    ]

    sums = [jnp.zeros((tok_rows, half), F32) for _ in range(2)]
    for k in range(hx_count):
        rows_k = jnp.concatenate([attended[g][k] for g in range(kv_heads)], axis=1)
        sums = [s + dot32(rows_k, m) for s, m in zip(sums, out_mats[k])]
    first = jnp.where(parity == 0, sums[0], sums[1])
    second = jnp.where(parity == 0, sums[1], sums[0])
    attn_sum = jnp.concatenate([first, second], axis=1)
    own_tokens = lax.dynamic_slice_in_dim(tokens, hx_index * width, width, 1)
    stream = (own_tokens.astype(F32) + attn_sum).astype(BF16)

    expert_out = None
    for c in range(CHUNKS):
        sent = dot32(pickers[c], stream).astype(BF16)
        sent = sent.reshape(ctx_count, exp_local, part, width)
        taken = lax.all_to_all(sent, "ctx", split_axis=0, concat_axis=0, tiled=True)
        shares = line_gather(taken.reshape(ctx_count * exp_local * part, width))
        rows = jnp.zeros((ctx_count * exp_local * part, full_width), BF16)
        for k in range(hx_count):
            source = (hx_index - k + hx_count) % hx_count
            rows = lax.dynamic_update_slice_in_dim(rows, shares[k], source * width, 1)
        normed2 = root_norm(rows, ffn_gain).reshape(ctx_count, exp_local, part, full_width)
        outs = []
        for e in range(exp_local):
            here = normed2[:, e].reshape(ctx_count * part, full_width)
            logits = dot32(here, w_router)
            column = jnp.arange(expert_count, dtype=jnp.int32) == ctx_index * exp_local + e
            score = jax.nn.sigmoid(jnp.sum(jnp.where(column[None, :], logits, 0.0), axis=-1))
            routed = (here.astype(F32) * score[:, None]).astype(BF16)
            gate_out = dot32(routed, w_gate[e])
            up_out = dot32(routed, w_up[e])
            hidden = (jax.nn.silu(gate_out) * up_out).astype(BF16)
            outs.append(dot32(hidden, w_down[e]).astype(BF16))
        reduced = jnp.stack(
            [line_scatter(o).reshape(ctx_count, part, width) for o in outs], axis=1
        )
        returned = lax.all_to_all(reduced, "ctx", split_axis=0, concat_axis=0, tiled=True)
        back = lax.dot_general(
            pickers[c],
            returned.reshape(expert_count * part, width),
            (((0,), (0,)), ((), ())),
            preferred_element_type=F32,
        )
        expert_out = back if expert_out is None else expert_out + back
    return (stream.astype(F32) + expert_out).astype(BF16)


def solution(mesh):
    return jax.shard_map(
        body,
        mesh=mesh,
        in_specs=(
            P("ctx", None),
            P(),
            P(),
            P("ctx", "hx"),
            P("ctx", "hx"),
            P("ctx", "hx"),
            P("hx", None),
            P(),
            P("ctx", None),
            P("ctx", None, "hx"),
            P("ctx", None, "hx"),
            P("ctx", "hx", None),
        ),
        out_specs=P("ctx", "hx"),
        check_vma=False,
    )
```

```python
import functools

import jax
import jax.numpy as jnp
import numpy as np
from jax import lax
from jax.experimental import pallas as pl
from jax.experimental.pallas import tpu as pltpu
from jax.sharding import PartitionSpec as P

HD = 128
epsilon = 1e-05
LOG2E = 1.4426950408889634
CHUNKS = 2
F32 = jnp.float32
BF16 = jnp.bfloat16


def dot32(left, right):
    return jnp.dot(left, right, preferred_element_type=F32)


def root_norm(values, gains):
    floats = values.astype(F32)
    inverse = lax.rsqrt(jnp.mean(floats * floats, axis=-1, keepdims=True) + epsilon)
    return (floats * inverse * gains.astype(F32)).astype(BF16)


def swap(value, axis, offset):
    count = lax.axis_size(axis)
    return lax.ppermute(value, axis, [(i, i ^ offset) for i in range(count)])


def near_blocks(block):
    return {offset: swap(block, "ctx", offset) for offset in (2, 4)}


def far_block(near):
    half = near[2].shape[0] // 2
    return swap(near[4][:half], "ctx", 2), swap(near[2][half:], "ctx", 4)


def after(value, *earlier):
    return lax.optimization_barrier((value,) + earlier)[0]


def ring_shift(values, k):
    count = lax.axis_size("hx")
    return lax.ppermute(values, "hx", [(j, (j + k) % count) for j in range(count)])


def line_pairs(step, spread):
    count = lax.axis_size("hx")
    pairs = [[], []]
    for j in range(count - 1):
        if (j >= step - 1) if spread else (j < step):
            pairs[j % 2].append((j, j + 1))
        if (j + 1 <= count - step) if spread else (j + 1 >= count - step):
            pairs[j % 2].append((j + 1, j))
    return pairs


def pass_on(values, pairs):
    return lax.ppermute(values, "hx", pairs) if pairs else jnp.zeros_like(values)


def line_gather(block):
    count = lax.axis_size("hx")
    even_in = odd_in = block
    earlier = ()
    for step in range(1, count):
        pairs = line_pairs(step, True)
        if earlier:
            even_in, odd_in = lax.optimization_barrier((even_in, odd_in) + tuple(earlier))[:2]
        even_in, odd_in = (
            pass_on(odd_in, pairs[0]) if pairs[0] else None,
            pass_on(even_in, pairs[1]) if pairs[1] else None,
        )
        even_in = odd_in if even_in is None else even_in
        odd_in = even_in if odd_in is None else odd_in
        even_in, odd_in = lax.optimization_barrier((even_in, odd_in))
        earlier = yield (even_in, odd_in)


def arrival_order(count):
    table = []
    for own in range(count):
        entries = []
        for step in range(1, count):
            for source, swap_is_odd in (
                (own - step, own % 2 == 0),
                (own + step, own % 2 == 1),
            ):
                if 0 <= source < count:
                    entries.append((source, 2 * (step - 1) + swap_is_odd))
        table.append(entries)
    return table


def line_scatter(values):
    count = lax.axis_size("hx")
    odd = lax.axis_index("hx") % 2 == 1
    even_in = odd_in = None
    for step in range(1, count):
        pairs = line_pairs(step, False)
        right, left = values[(count - step) % count], values[step % count]
        even_out, odd_out = jnp.where(odd, left, right), jnp.where(odd, right, left)
        if step > 1:
            even_out = (even_out.astype(F32) + odd_in.astype(F32)).astype(BF16)
            odd_out = (odd_out.astype(F32) + even_in.astype(F32)).astype(BF16)
            earlier = tuple(earlier or ())
            even_out, odd_out = lax.optimization_barrier((even_out, odd_out) + earlier)[:2]
        even_in, odd_in = pass_on(even_out, pairs[0]), pass_on(odd_out, pairs[1])
        if step < count - 1:
            earlier = yield (even_in, odd_in)
    total = values[0].astype(F32)
    if count > 1:
        total = total + even_in.astype(F32) + odd_in.astype(F32)
    yield total.astype(BF16)


SMALL = pl.CostEstimate(flops=0, bytes_accessed=4096, transcendentals=0)
VMEM_LIMIT = 48 * 1024 * 1024


def norm_kernel(values_ref, gains_ref, out_ref):
    floats = values_ref[...].astype(F32)
    inverse = lax.rsqrt(jnp.mean(floats * floats, axis=-1, keepdims=True) + epsilon)
    out_ref[...] = (floats * inverse * gains_ref[...].astype(F32)).astype(BF16)


def norm_rows(values, gains):
    rows, columns = values.shape
    tile = min(rows, 128)
    return pl.pallas_call(
        norm_kernel,
        out_shape=jax.ShapeDtypeStruct((rows, columns), BF16),
        grid=(rows // tile,),
        in_specs=[
            pl.BlockSpec((tile, columns), lambda r: (r, 0)),
            pl.BlockSpec((1, columns), lambda r: (0, 0)),
        ],
        out_specs=pl.BlockSpec((tile, columns), lambda r: (r, 0)),
        compiler_params=pltpu.CompilerParams(vmem_limit_bytes=VMEM_LIMIT),
        cost_estimate=SMALL,
        name="norm_rows",
    )(values, gains.reshape(1, columns))


def choose(code, refs):
    value = refs[0][...]
    for number in range(1, len(refs)):
        value = jnp.where(code == number, refs[number][...], value)
    return value


def sum_dots_kernel(codes_ref, *refs, lefts, splits, added):
    left, right, chosen = refs[:lefts], refs[lefts : lefts + sum(splits)], refs[-1]
    out_ref = refs[-2]

    @pl.when(pl.program_id(0) == 0)
    def _():
        for k in range(len(splits)):
            chosen[k] = choose(codes_ref[k], left)

    total = None
    for more in refs[lefts + sum(splits) : lefts + sum(splits) + added]:
        part = more[...].astype(F32)
        total = part if total is None else total + part
    number = 0
    for k, split in enumerate(splits):
        at = 0
        for _ in range(split):
            rows = right[number].shape[0]
            part = dot32(chosen[k, :, at : at + rows], right[number][...])
            total = part if total is None else total + part
            at += rows
            number += 1
    out_ref[...] = total.astype(out_ref.dtype)


def sum_dots(codes, lefts, rights, added):
    rows, columns = lefts[0].shape[0], rights[0][0].shape[1]
    tile = 256 if columns % 256 == 0 else 128
    flat = [m for mats in rights for m in mats]
    out = pl.BlockSpec((rows, tile), lambda c, s: (0, c))
    return pl.pallas_call(
        functools.partial(
            sum_dots_kernel,
            lefts=len(lefts),
            splits=tuple(len(mats) for mats in rights),
            added=len(added),
        ),
        out_shape=jax.ShapeDtypeStruct((rows, columns), BF16),
        grid_spec=pltpu.PrefetchScalarGridSpec(
            num_scalar_prefetch=1,
            grid=(columns // tile,),
            in_specs=[pl.BlockSpec(m.shape, lambda c, s: (0, 0)) for m in lefts]
            + [pl.BlockSpec((m.shape[0], tile), lambda c, s: (0, c)) for m in flat]
            + [out] * len(added),
            out_specs=out,
            scratch_shapes=[pltpu.VMEM((len(rights),) + lefts[0].shape, BF16)],
        ),
        compiler_params=pltpu.CompilerParams(vmem_limit_bytes=VMEM_LIMIT),
        cost_estimate=SMALL,
        name="sum_dots",
    )(codes, *lefts, *flat, *added)


def project_kernel(places_ref, *refs, count, mats, added):
    del places_ref
    outs = refs[len(refs) - count :]
    for j in range(count):
        total = refs[(count + 1) * mats + j][...] if added else None
        for k in range(mats):
            part = dot32(refs[j * mats + k][...], refs[count * mats + k][...])
            total = part if total is None else total + part
        outs[j][...] = total.astype(outs[j].dtype)


def project(values, mats, places, totals, dtype):
    rows = values[0].shape[0]
    columns = mats[0].shape[1]
    whole = pl.BlockSpec((rows, columns), lambda g, s: (0, 0))

    def columns_at(k):
        return pl.BlockSpec((rows, mats[k].shape[0]), lambda g, s: (0, s[k]))

    return pl.pallas_call(
        functools.partial(
            project_kernel, count=len(values), mats=len(mats), added=totals is not None
        ),
        out_shape=[jax.ShapeDtypeStruct((rows, columns), dtype) for _ in values],
        grid_spec=pltpu.PrefetchScalarGridSpec(
            num_scalar_prefetch=1,
            grid=(1,),
            in_specs=[columns_at(k) for _ in values for k in range(len(mats))]
            + [pl.BlockSpec(m.shape, lambda g, s: (0, 0)) for m in mats]
            + [whole] * len(totals or ()),
            out_specs=[whole] * len(values),
        ),
        compiler_params=pltpu.CompilerParams(vmem_limit_bytes=VMEM_LIMIT),
        cost_estimate=SMALL,
        name="project",
    )(
        jnp.stack(places).astype(jnp.int32),
        *[v for v in values for _ in mats],
        *mats,
        *(totals or ()),
    )


def attend_kernel(places_ref, query_ref, *refs, group_size):
    *pieces, out_ref, held = refs
    rows = query_ref.shape[0]
    own = places_ref[0]
    scale = HD ** (-0.5) * LOG2E
    queries = [query_ref[:, g * HD : (g + 1) * HD] for g in range(group_size)]

    number = 1
    for piece in pieces:
        for start in range(0, piece.shape[0], rows):
            to = pl.multiple_of(places_ref[number] * rows, rows)
            held[pl.ds(to, rows), :] = piece[start : start + rows, :]
            number += 1

    def block(start, states, masked):
        keys = held[pl.ds(start, rows), :HD]
        values = held[pl.ds(start, rows), HD:]
        states_out = []
        for query, (top, total, acc) in zip(queries, states):
            scores = lax.dot_general(
                keys, query, (((1,), (1,)), ((), ())), preferred_element_type=F32
            )
            if masked:
                key_at = lax.broadcasted_iota(jnp.int32, scores.shape, 0)
                query_at = lax.broadcasted_iota(jnp.int32, scores.shape, 1)
                scores = jnp.where(key_at <= query_at, scores, -1e30)
            new_top = jnp.maximum(top, jnp.max(scores, axis=0, keepdims=True))
            weights = jnp.exp2((scores - new_top) * scale)
            factor = jnp.exp2((top - new_top) * scale)
            total = total * factor + jnp.sum(weights, axis=0, keepdims=True)
            mixed = lax.dot_general(
                values,
                weights.astype(BF16),
                (((0,), (0,)), ((), ())),
                preferred_element_type=F32,
            )
            states_out.append((new_top, total, acc * factor + mixed))
        return tuple(states_out)

    start_state = tuple(
        (
            jnp.full((1, rows), -1e30, F32),
            jnp.zeros((1, rows), F32),
            jnp.zeros((HD, rows), F32),
        )
        for _ in range(group_size)
    )
    states = block(pl.multiple_of(own * rows, rows), start_state, True)
    states = lax.fori_loop(
        0, own, lambda j, held: block(pl.multiple_of(j * rows, rows), held, False), states
    )
    for g, (_, total, acc) in enumerate(states):
        out_ref[:, g * HD : (g + 1) * HD] = (acc / total).T.astype(BF16)


def attend(own, queries, pieces, places):
    rows, width = queries.shape
    count = sum(p.shape[0] for p in pieces)
    whole = pl.BlockSpec((rows, width), lambda g, s: (0, 0))
    return pl.pallas_call(
        functools.partial(attend_kernel, group_size=width // HD),
        out_shape=jax.ShapeDtypeStruct((rows, width), BF16),
        grid_spec=pltpu.PrefetchScalarGridSpec(
            num_scalar_prefetch=1,
            grid=(1,),
            in_specs=[whole] + [pl.BlockSpec(p.shape, lambda g, s: (0, 0)) for p in pieces],
            out_specs=whole,
            scratch_shapes=[pltpu.VMEM((count, 2 * HD), BF16)],
        ),
        compiler_params=pltpu.CompilerParams(vmem_limit_bytes=VMEM_LIMIT),
        cost_estimate=pl.CostEstimate(
            flops=4 * rows * count * width,
            bytes_accessed=4 * count * HD,
            transcendentals=rows * count * width // HD,
        ),
        name="attend",
    )(jnp.stack([own] + places).astype(jnp.int32), queries, *pieces)


def hidden_tile(hidden):
    return 256 if hidden % 256 == 0 else 128


def scale_share(code_ref, shares, gain_ref, router_ref, scaled_ref):
    value = choose(code_ref[1], shares).astype(F32)
    scaled = (value * gain_ref[...].astype(F32)).astype(BF16)
    scaled_ref[...] = scaled

    def lanes(wide):
        return sum(wide[:, at : at + 128] for at in range(0, wide.shape[1], 128))

    return lanes(value * value), lanes(scaled.astype(F32) * router_ref[...].astype(F32))


def share_kernel(code_ref, *refs, shares, added):
    gain_ref, router_ref, gate_ref, up_ref = refs[shares : shares + 4]
    totals, outs, scaled = refs[shares + 4 : -5], refs[-5:-1], refs[-1]

    @pl.when(pl.program_id(0) == 0)
    def _():
        parts = scale_share(code_ref, refs[:shares], gain_ref, router_ref, scaled)
        for number, part in enumerate(parts):
            outs[2 + number][...] = part + totals[2 + number][...] if added else part

    for number, mat in enumerate((gate_ref, up_ref)):
        part = dot32(scaled[...], mat[0])
        outs[number][...] = part + totals[number][...] if added else part


def expert_share(code, shares, gains, router_row, w_gate, w_up, totals, which):
    rows, width = shares[0].shape
    hidden = w_gate.shape[2]
    tile = hidden_tile(hidden)
    sums = [pl.BlockSpec((rows, tile), lambda t, s: (0, t))] * 2 + [
        pl.BlockSpec((rows, 128), lambda t, s: (0, 0))
    ] * 2
    return pl.pallas_call(
        functools.partial(share_kernel, shares=len(shares), added=totals is not None),
        out_shape=[jax.ShapeDtypeStruct((rows, n), F32) for n in (hidden, hidden, 128, 128)],
        grid_spec=pltpu.PrefetchScalarGridSpec(
            num_scalar_prefetch=1,
            grid=(hidden // tile,),
            in_specs=[pl.BlockSpec((rows, width), lambda t, s: (0, 0))] * len(shares)
            + [pl.BlockSpec((1, width), lambda t, s: (0, s[0]))] * 2
            + [pl.BlockSpec((1, width, tile), lambda t, s: (which, s[0], t))] * 2
            + (sums if totals is not None else []),
            out_specs=sums,
            scratch_shapes=[pltpu.VMEM((rows, width), BF16)],
        ),
        compiler_params=pltpu.CompilerParams(vmem_limit_bytes=VMEM_LIMIT),
        cost_estimate=SMALL,
        name="expert_share",
    )(code, *shares, gains, router_row, w_gate, w_up, *(totals or ()))


def finish_kernel(code_ref, *refs, shares, tiles, full_width):
    gain_ref, router_ref, gate_ref, up_ref = refs[shares : shares + 4]
    gate_sum, up_sum, squares_sum, logits_sum, down_ref, out_ref = refs[shares + 4 : shares + 10]
    scaled, factor, hidden = refs[-3:]
    step = pl.program_id(0)

    @pl.when(step == 0)
    def _():
        squares, logits = scale_share(code_ref, refs[:shares], gain_ref, router_ref, scaled)
        squares = jnp.sum(squares + squares_sum[...], axis=-1, keepdims=True)
        logit = jnp.sum(logits + logits_sum[...], axis=-1, keepdims=True)
        inverse = lax.rsqrt(squares / full_width + epsilon)
        score = 1.0 / (1.0 + jnp.exp(-logit * inverse))
        factor[...] = jnp.broadcast_to(inverse * score, factor.shape)

    @pl.when(step < tiles)
    def _():
        scale = factor[:, :1]
        gate = (dot32(scaled[...], gate_ref[0]) + gate_sum[...]) * scale
        up = (dot32(scaled[...], up_ref[0]) + up_sum[...]) * scale
        hidden[step] = (gate / (1.0 + jnp.exp(-gate)) * up).astype(BF16)

    @pl.when(step >= tiles)
    def _():
        tile = hidden.shape[2]
        total = None
        for t in range(tiles):
            part = dot32(hidden[t], down_ref[0, t * tile : (t + 1) * tile, :])
            total = part if total is None else total + part
        out_ref[0] = total.astype(BF16)


def expert_finish(code, shares, gains, router_row, w_gate, w_up, totals, w_down, which):
    rows, width = shares[0].shape
    hidden = w_gate.shape[2]
    count = w_down.shape[2] // width
    tile = hidden_tile(hidden)
    tiles = hidden // tile

    def at(t):
        return jnp.minimum(t, tiles - 1)

    def after_tiles(t):
        return jnp.maximum(t - tiles, 0)

    return pl.pallas_call(
        functools.partial(
            finish_kernel, shares=len(shares), tiles=tiles, full_width=w_down.shape[2]
        ),
        out_shape=jax.ShapeDtypeStruct((count, rows, width), BF16),
        grid_spec=pltpu.PrefetchScalarGridSpec(
            num_scalar_prefetch=1,
            grid=(tiles + count,),
            in_specs=[pl.BlockSpec((rows, width), lambda t, s: (0, 0))] * len(shares)
            + [pl.BlockSpec((1, width), lambda t, s: (0, s[0]))] * 2
            + [pl.BlockSpec((1, width, tile), lambda t, s: (which, s[0], at(t)))] * 2
            + [pl.BlockSpec((rows, tile), lambda t, s: (0, at(t)))] * 2
            + [pl.BlockSpec((rows, 128), lambda t, s: (0, 0))] * 2
            + [
                pl.BlockSpec(
                    (1, hidden, width),
                    lambda t, s: (which, 0, lax.rem(s[2] + after_tiles(t), count)),
                )
            ],
            out_specs=pl.BlockSpec((1, rows, width), lambda t, s: (after_tiles(t), 0, 0)),
            scratch_shapes=[
                pltpu.VMEM((rows, width), BF16),
                pltpu.VMEM((rows, 128), F32),
                pltpu.VMEM((tiles, rows, tile), BF16),
            ],
        ),
        compiler_params=pltpu.CompilerParams(vmem_limit_bytes=VMEM_LIMIT),
        cost_estimate=SMALL,
        name="expert_finish",
    )(code, *shares, gains, router_row, w_gate, w_up, *totals, w_down)


def attention_share(tokens, own_tokens, attn_gain, w_query, w_key, w_value, w_out):
    ctx_index = lax.axis_index("ctx")
    kv_heads = w_key.shape[1] // HD
    group_width = w_query.shape[1] // kv_heads
    normed = root_norm(tokens, attn_gain)
    queries, keys, values = (
        dot32(normed, lax.all_gather(w, "ctx", axis=0, tiled=True)).astype(BF16)
        for w in (w_query, w_key, w_value)
    )
    keys = lax.all_gather(keys, "ctx", axis=0, tiled=True)
    values = lax.all_gather(values, "ctx", axis=0, tiled=True)
    places = [jnp.int32(b) for b in range(lax.axis_size("ctx"))]
    attended = []
    for g in range(kv_heads):
        head = slice(g * HD, (g + 1) * HD)
        piece = jnp.concatenate([keys[:, head], values[:, head]], axis=1)
        query = queries[:, g * group_width : (g + 1) * group_width]
        attended.append(attend(ctx_index, query, [piece], places))
    partial = dot32(jnp.concatenate(attended, axis=1), w_out).astype(BF16)
    attn_sum = lax.psum_scatter(partial, "hx", scatter_dimension=1, tiled=True)
    return (own_tokens.astype(F32) + attn_sum.astype(F32)).astype(BF16)


def paired_attention_share(tokens, own_tokens, attn_gain, w_query, w_key, w_value, w_out):
    ctx_count = lax.axis_size("ctx")
    hx_count = lax.axis_size("hx")
    ctx_index = lax.axis_index("ctx")
    hx_index = lax.axis_index("hx")
    parity = ctx_index % 2
    tok_rows, full_width = tokens.shape
    width = full_width // hx_count
    kv_heads = w_key.shape[1] // HD // 2
    kv_width = kv_heads * HD
    query_width = w_query.shape[1] // 2
    group_width = query_width // kv_heads

    def side(matrix, which, size, axis=1):
        return lax.dynamic_slice_in_dim(matrix, which * size, size, axis)

    own_kv = jnp.concatenate([side(m, parity, kv_width) for m in (w_key, w_value)], axis=1)
    own_query = side(w_query, parity, query_width)
    other_kv = jnp.concatenate([side(m, 1 - parity, kv_width) for m in (w_key, w_value)], axis=1)
    take = swap(other_kv, "ctx", 1)
    take_query = swap(side(w_query, after(1 - parity, take), query_width), "ctx", 1)
    other_tokens = swap(after(tokens, take_query), "ctx", 1)
    middle = hx_count // 2 if hx_count > 2 else 0
    half_rows = query_width // 2
    moves = []
    for k in [k for k in range(1, hx_count) if k != middle] + [middle] * (middle > 0):
        pieces = ((0, half_rows), (half_rows, half_rows)) if k == middle else ((0, query_width),)
        moves += [(k, *piece) for piece in pieces]

    def out_block(k, first_row, size, row_at):
        place = (row_at + first_row, (hx_index + k) % hx_count * width)
        return lax.dynamic_slice(w_out, place, (size, width))

    out_parts = {}

    def next_block(*earlier):
        if not moves:
            return None
        k, first_row, size = moves.pop(0)
        return k, out_block(k, first_row, size, after(parity * query_width, *earlier))

    def move(sent, *earlier):
        if sent is None:
            return ()
        k, block = sent
        block = after(block, *earlier) if earlier else block
        out_parts.setdefault(k, []).append(ring_shift(block, k))
        return (out_parts[k][-1],)

    def ready(sent):
        return () if sent is None else (sent[1],)

    def in_order(own, other):
        pair = (jnp.where(parity == 0, own, other), jnp.where(parity == 0, other, own))
        return jnp.concatenate(pair, axis=0)

    kv_mats = in_order(own_kv, take)
    query_mats = in_order(own_query, take_query)

    def together(arrived, *others):
        flat, tree = jax.tree.flatten(arrived)
        flat = lax.optimization_barrier(tuple(flat) + others)
        return jax.tree.unflatten(tree, flat[: len(flat) - len(others)])

    def pair_at(offset):
        return (ctx_index ^ offset) // 2

    def project_near(mats, near):
        places = [pair_at(0), pair_at(2), pair_at(4)]
        return project(normed, [mats, near[2], near[4]], places, None, F32)

    def project_far(far, total):
        places = [2 * pair_at(6), 2 * pair_at(6) + 1]
        return project(normed, list(far), places, total, BF16)

    normed = [norm_rows(t, attn_gain) for t in (tokens, other_tokens)]
    sent = next_block(take)
    following = next_block(take_query)
    kv_near = together(
        near_blocks(kv_mats), *move(sent), *ready(following), other_tokens, normed[0]
    )
    first = kv_near[2]
    sent, following = following, next_block(first)
    kv_total = project_near(kv_mats, kv_near)
    kv_far, query_near, kv_total = together(
        (far_block(kv_near), near_blocks(after(query_mats, first)), kv_total),
        *move(sent, first),
        *ready(following),
    )
    before, first = first, query_near[2]
    sent, following = following, next_block(before)
    kv_pair = jnp.concatenate(project_far(kv_far, kv_total), axis=0)
    query_total = project_near(query_mats, query_near)
    block_near, query_far, query_total = together(
        (near_blocks(kv_pair), far_block(query_near), query_total),
        *move(sent, first),
        *ready(following),
    )
    first = block_near[2]
    last_move = move(following, first)
    out_parts[0] = [out_block(0, 0, query_width, after(parity * query_width, first))]
    block_far = far_block(block_near)
    queries = project_far(query_far, query_total)
    pieces = [kv_pair, block_near[2], block_near[4], *block_far]
    places = [ctx_index ^ o ^ j for o in (0, 2, 4, 6) for j in (0, 1)]

    def head(piece, g):
        if kv_heads == 1:
            return piece
        columns = [piece[:, h * HD : (h + 1) * HD] for h in (g, kv_heads + g)]
        return jnp.concatenate(columns, axis=1)

    lefts = {}
    for j in (1, 0):
        attended = [
            attend(
                ctx_index ^ j,
                queries[j][:, g * group_width : (g + 1) * group_width],
                [head(piece, g) for piece in pieces],
                places,
            )
            for g in range(kv_heads)
        ]
        attended = jnp.concatenate(attended, axis=1)
        if j == 1:
            attended = after(attended, *last_move) if last_move else attended
        lefts[j] = [attended] + [x for pair in line_gather(attended) for x in pair]
    flat = lax.optimization_barrier(tuple(lefts[1]) + tuple(lefts[0]))
    lefts = {1: flat[: len(lefts[1])], 0: flat[len(lefts[1]) :]}
    table = np.zeros((hx_count, hx_count), np.int32)
    for own, entries in enumerate(arrival_order(hx_count)):
        for source, number in entries:
            table[own, (own - source) % hx_count] = 1 + number
    codes = jnp.asarray(table)[hx_index]
    rights = [out_parts[k] for k in range(hx_count)]
    given = swap(sum_dots(codes, lefts[1], rights, ()), "ctx", 1)
    return sum_dots(codes, lefts[0], rights, (given, own_tokens))


def body(
    tokens,
    attn_gain,
    ffn_gain,
    w_query,
    w_key,
    w_value,
    w_out,
    w_router,
    routes,
    w_gate,
    w_up,
    w_down,
):
    ctx_count = lax.axis_size("ctx")
    hx_count = lax.axis_size("hx")
    ctx_index = lax.axis_index("ctx")
    hx_index = lax.axis_index("hx")
    tok_rows, full_width = tokens.shape
    width = full_width // hx_count
    expert_count = w_router.shape[1]

    chosen = routes[:, 0]
    onehot = chosen[:, None] == jnp.arange(expert_count, dtype=jnp.int32)[None, :]
    counts = jnp.cumsum(onehot.astype(jnp.int32), axis=0)
    position = jnp.sum(jnp.where(onehot, counts, 0), axis=-1) - 1
    capacity = tok_rows // 8
    part = capacity // CHUNKS
    exp_local = w_gate.shape[0]
    slot_expert = jnp.arange(expert_count * part, dtype=jnp.int32) // part
    slot_place = jnp.arange(expert_count * part, dtype=jnp.int32) % part
    pickers = [
        (
            (slot_expert[:, None] == chosen[None, :])
            & (slot_place[:, None] + c * part == position[None, :])
        ).astype(BF16)
        for c in range(CHUNKS)
    ]

    paired = ctx_count // 2 == 4 and (w_key.shape[1] // HD) % 2 == 0
    share_of = paired_attention_share if paired else attention_share
    own_tokens = lax.dynamic_slice_in_dim(tokens, hx_index * width, width, 1)
    stream = share_of(tokens, own_tokens, attn_gain, w_query, w_key, w_value, w_out)

    gains = ffn_gain.reshape(1, full_width)
    router_rows = w_router.T
    order = arrival_order(hx_count)
    codes = [jnp.stack([hx_index, jnp.int32(0), hx_index]).astype(jnp.int32)]
    for t in range(hx_count - 1):
        found = jnp.asarray(np.array([entries[t] for entries in order], np.int32))[hx_index]
        codes.append(jnp.concatenate([found, codes[0][2:]]))

    def give_back(c, reduced):
        reduced = jnp.stack([r.reshape(ctx_count, part, width) for r in reduced], axis=1)
        returned = lax.all_to_all(reduced, "ctx", split_axis=0, concat_axis=0, tiled=True)
        return returned.reshape(expert_count * part, width)

    returned = []
    scatter, arrived, reached = None, (), ()
    for c in range(CHUNKS):
        sent = dot32(pickers[c], stream).astype(BF16)
        sent = sent.reshape(ctx_count, exp_local, part, width)
        taken = lax.all_to_all(sent, "ctx", split_axis=0, concat_axis=0, tiled=True)
        if reached:
            taken = after(taken, *reached)
        taken = taken.reshape(ctx_count, exp_local, part, width)
        taken = taken.swapaxes(0, 1).reshape(exp_local * ctx_count * part, width)
        gather = line_gather(taken)
        rows = [slice(e * ctx_count * part, (e + 1) * ctx_count * part) for e in range(exp_local)]
        router = [
            lax.dynamic_slice_in_dim(router_rows, ctx_index * exp_local + e, 1, 0)
            for e in range(exp_local)
        ]
        shares = [taken]
        totals = [None] * exp_local
        for t in range(hx_count - 1):
            earlier = [x for sums in totals if sums for x in sums[2:]] + shares[-1:] * (t == 0)
            if t == hx_count - 2:
                earlier += arrived
            pair = next(gather) if t == 0 else gather.send(earlier)
            totals = [
                expert_share(
                    codes[t], [x[rows[e]] for x in shares[t > 0 :]], gains, router[e], w_gate, w_up, totals[e], e
                )
                for e in range(exp_local)
            ]
            reached = pair
            if scatter and t == hx_count - 2:
                arrived = [x for sums in scatter for x in next(sums)]
                pair = lax.optimization_barrier(tuple(pair) + tuple(arrived))[:2]
            shares = shares + list(pair)
        outs = [
            expert_finish(
                codes[-1], [x[rows[e]] for x in shares[1:]], gains, router[e], w_gate, w_up, totals[e], w_down, e
            )
            for e in range(exp_local)
        ]
        reduced = None
        if scatter:
            for _ in range(hx_count - 4):
                [next(sums) for sums in scatter]
            reduced = [next(sums) for sums in scatter]
            outs = [after(o, *reduced) for o in outs]
        scatter = [line_scatter(o) for o in outs]
        arrived = [x for sums in scatter for x in next(sums)]
        if reduced:
            returned.append(give_back(c - 1, [after(r, *arrived) for r in reduced]))
    for step in range(hx_count - 3):
        [next(sums) for sums in scatter]
    reduced = [sums.send(returned) if hx_count > 2 else next(sums) for sums in scatter]
    returned.append(give_back(CHUNKS - 1, reduced))
    expert_out = sum(
        lax.dot_general(p, r, (((0,), (0,)), ((), ())), preferred_element_type=F32)
        for p, r in zip(pickers, returned)
    )
    return (stream.astype(F32) + expert_out).astype(BF16)


def solution(mesh):
    return jax.shard_map(
        body,
        mesh=mesh,
        in_specs=(
            P("ctx", None),
            P(),
            P(),
            P("ctx", "hx"),
            P("ctx", "hx"),
            P("ctx", "hx"),
            P("hx", None),
            P(),
            P("ctx", None),
            P("ctx", None, "hx"),
            P("ctx", None, "hx"),
            P("ctx", "hx", None),
        ),
        out_specs=P("ctx", "hx"),
        check_vma=False,
    )
```

```python
import functools

import jax
import jax.numpy as jnp
import numpy as np
from jax import lax
from jax.experimental import pallas as pl
from jax.experimental.pallas import tpu as pltpu
from jax.sharding import PartitionSpec as P

HD = 128
epsilon = 1e-05
LOG2E = 1.4426950408889634
CHUNKS = 2
F32 = jnp.float32
BF16 = jnp.bfloat16


def dot32(left, right):
    return jnp.dot(left, right, preferred_element_type=F32)


def root_norm(values, gains):
    floats = values.astype(F32)
    inverse = lax.rsqrt(jnp.mean(floats * floats, axis=-1, keepdims=True) + epsilon)
    return (floats * inverse * gains.astype(F32)).astype(BF16)


def swap(value, axis, offset):
    count = lax.axis_size(axis)
    return lax.ppermute(value, axis, [(i, i ^ offset) for i in range(count)])


def near_blocks(block):
    return {offset: swap(block, "ctx", offset) for offset in (2, 4)}


def far_block(near):
    half = near[2].shape[0] // 2
    return swap(near[4][:half], "ctx", 2), swap(near[2][half:], "ctx", 4)


def after(value, *earlier):
    return lax.optimization_barrier((value,) + earlier)[0]


def ring_shift(values, k):
    count = lax.axis_size("hx")
    return lax.ppermute(values, "hx", [(j, (j + k) % count) for j in range(count)])


def line_pairs(step, spread):
    count = lax.axis_size("hx")
    pairs = [[], []]
    for j in range(count - 1):
        if (j >= step - 1) if spread else (j < step):
            pairs[j % 2].append((j, j + 1))
        if (j + 1 <= count - step) if spread else (j + 1 >= count - step):
            pairs[j % 2].append((j + 1, j))
    return pairs


def pass_on(values, pairs):
    return lax.ppermute(values, "hx", pairs) if pairs else jnp.zeros_like(values)


def line_gather(block):
    count = lax.axis_size("hx")
    even_in = odd_in = block
    earlier = ()
    for step in range(1, count):
        pairs = line_pairs(step, True)
        if earlier:
            even_in, odd_in = lax.optimization_barrier((even_in, odd_in) + tuple(earlier))[:2]
        even_in, odd_in = (
            pass_on(odd_in, pairs[0]) if pairs[0] else None,
            pass_on(even_in, pairs[1]) if pairs[1] else None,
        )
        even_in = odd_in if even_in is None else even_in
        odd_in = even_in if odd_in is None else odd_in
        even_in, odd_in = lax.optimization_barrier((even_in, odd_in))
        earlier = yield (even_in, odd_in)


def arrival_order(count):
    table = []
    for own in range(count):
        entries = []
        for step in range(1, count):
            for source, swap_is_odd in (
                (own - step, own % 2 == 0),
                (own + step, own % 2 == 1),
            ):
                if 0 <= source < count:
                    entries.append((source, 2 * (step - 1) + swap_is_odd))
        table.append(entries)
    return table


def line_scatter(values):
    count = lax.axis_size("hx")
    odd = lax.axis_index("hx") % 2 == 1
    even_in = odd_in = None
    for step in range(1, count):
        pairs = line_pairs(step, False)
        right, left = values[(count - step) % count], values[step % count]
        even_out, odd_out = jnp.where(odd, left, right), jnp.where(odd, right, left)
        if step > 1:
            even_out = (even_out.astype(F32) + odd_in.astype(F32)).astype(BF16)
            odd_out = (odd_out.astype(F32) + even_in.astype(F32)).astype(BF16)
            earlier = tuple(earlier or ())
            even_out, odd_out = lax.optimization_barrier((even_out, odd_out) + earlier)[:2]
        even_in, odd_in = pass_on(even_out, pairs[0]), pass_on(odd_out, pairs[1])
        if step < count - 1:
            earlier = yield (even_in, odd_in)
    total = values[0].astype(F32)
    if count > 1:
        total = total + even_in.astype(F32) + odd_in.astype(F32)
    yield total.astype(BF16)


SMALL = pl.CostEstimate(flops=0, bytes_accessed=4096, transcendentals=0)
VMEM_LIMIT = 48 * 1024 * 1024


def norm_kernel(values_ref, gains_ref, out_ref):
    floats = values_ref[...].astype(F32)
    inverse = lax.rsqrt(jnp.mean(floats * floats, axis=-1, keepdims=True) + epsilon)
    out_ref[...] = (floats * inverse * gains_ref[...].astype(F32)).astype(BF16)


def norm_rows(values, gains):
    rows, columns = values.shape
    tile = min(rows, 128)
    return pl.pallas_call(
        norm_kernel,
        out_shape=jax.ShapeDtypeStruct((rows, columns), BF16),
        grid=(rows // tile,),
        in_specs=[
            pl.BlockSpec((tile, columns), lambda r: (r, 0)),
            pl.BlockSpec((1, columns), lambda r: (0, 0)),
        ],
        out_specs=pl.BlockSpec((tile, columns), lambda r: (r, 0)),
        compiler_params=pltpu.CompilerParams(vmem_limit_bytes=VMEM_LIMIT),
        cost_estimate=SMALL,
        name="norm_rows",
    )(values, gains.reshape(1, columns))


def choose(code, refs, numbers=None):
    first, *others = numbers or range(len(refs))
    value = refs[first][...]
    for number in others:
        value = jnp.where(code == number, refs[number][...], value)
    return value


def sum_dots_kernel(codes_ref, *refs, lefts, splits, added, numbers):
    left, right, chosen = refs[:lefts], refs[lefts : lefts + sum(splits)], refs[-1]
    out_ref = refs[-2]

    @pl.when(pl.program_id(0) == 0)
    def _():
        for k in range(len(splits)):
            chosen[k] = choose(codes_ref[k], left, numbers[k])

    total = None
    for more in refs[lefts + sum(splits) : lefts + sum(splits) + added]:
        part = more[...].astype(F32)
        total = part if total is None else total + part
    number = 0
    for k, split in enumerate(splits):
        at = 0
        for _ in range(split):
            rows = right[number].shape[0]
            part = dot32(chosen[k, :, at : at + rows], right[number][...])
            total = part if total is None else total + part
            at += rows
            number += 1
    out_ref[...] = total.astype(out_ref.dtype)


def sum_dots(codes, numbers, lefts, rights, added):
    rows, columns = lefts[0].shape[0], rights[0][0].shape[1]
    tile = 256 if columns % 256 == 0 else 128
    flat = [m for mats in rights for m in mats]
    out = pl.BlockSpec((rows, tile), lambda c, s: (0, c))
    return pl.pallas_call(
        functools.partial(
            sum_dots_kernel,
            lefts=len(lefts),
            splits=tuple(len(mats) for mats in rights),
            added=len(added),
            numbers=numbers,
        ),
        out_shape=jax.ShapeDtypeStruct((rows, columns), BF16),
        grid_spec=pltpu.PrefetchScalarGridSpec(
            num_scalar_prefetch=1,
            grid=(columns // tile,),
            in_specs=[pl.BlockSpec(m.shape, lambda c, s: (0, 0)) for m in lefts]
            + [pl.BlockSpec((m.shape[0], tile), lambda c, s: (0, c)) for m in flat]
            + [out] * len(added),
            out_specs=out,
            scratch_shapes=[pltpu.VMEM((len(rights),) + lefts[0].shape, BF16)],
        ),
        compiler_params=pltpu.CompilerParams(vmem_limit_bytes=VMEM_LIMIT),
        cost_estimate=SMALL,
        name="sum_dots",
    )(codes, *lefts, *flat, *added)


def project_kernel(places_ref, *refs, count, mats, added):
    del places_ref
    outs = refs[len(refs) - count :]
    for j in range(count):
        total = refs[(count + 1) * mats + j][...] if added else None
        for k in range(mats):
            part = dot32(refs[j * mats + k][...], refs[count * mats + k][...])
            total = part if total is None else total + part
        outs[j][...] = total.astype(outs[j].dtype)


def project(values, mats, places, totals, dtype):
    rows = values[0].shape[0]
    columns = mats[0].shape[1]
    whole = pl.BlockSpec((rows, columns), lambda g, s: (0, 0))

    def columns_at(k):
        return pl.BlockSpec((rows, mats[k].shape[0]), lambda g, s: (0, s[k]))

    return pl.pallas_call(
        functools.partial(
            project_kernel, count=len(values), mats=len(mats), added=totals is not None
        ),
        out_shape=[jax.ShapeDtypeStruct((rows, columns), dtype) for _ in values],
        grid_spec=pltpu.PrefetchScalarGridSpec(
            num_scalar_prefetch=1,
            grid=(1,),
            in_specs=[columns_at(k) for _ in values for k in range(len(mats))]
            + [pl.BlockSpec(m.shape, lambda g, s: (0, 0)) for m in mats]
            + [whole] * len(totals or ()),
            out_specs=[whole] * len(values),
        ),
        compiler_params=pltpu.CompilerParams(vmem_limit_bytes=VMEM_LIMIT),
        cost_estimate=SMALL,
        name="project",
    )(
        jnp.stack(places).astype(jnp.int32),
        *[v for v in values for _ in mats],
        *mats,
        *(totals or ()),
    )


def attend_kernel(places_ref, query_ref, *refs, group_size):
    *pieces, out_ref, held = refs
    rows = query_ref.shape[0]
    own = places_ref[0]
    scale = HD ** (-0.5) * LOG2E
    queries = jnp.concatenate(
        [query_ref[:, g * HD : (g + 1) * HD] for g in range(group_size)], axis=0
    )

    number = 1
    for piece in pieces:
        for start in range(0, piece.shape[0], rows):
            to = pl.multiple_of(places_ref[number] * rows, rows)
            held[pl.ds(to, rows), :] = piece[start : start + rows, :]
            number += 1

    def block(first, count, state, masked=False):
        at = pl.ds(pl.multiple_of(first * rows, rows), count * rows)
        top, total, acc = state
        scores = lax.dot_general(
            held[at, :HD], queries, (((1,), (1,)), ((), ())), preferred_element_type=F32
        )
        if masked:
            key_at = lax.broadcasted_iota(jnp.int32, scores.shape, 0)
            query_at = lax.broadcasted_iota(jnp.int32, scores.shape, 1) % rows
            scores = jnp.where(key_at <= query_at, scores, -1e30)
        new_top = jnp.maximum(top, jnp.max(scores, axis=0, keepdims=True))
        weights = jnp.exp2((scores - new_top) * scale)
        factor = jnp.exp2((top - new_top) * scale)
        total = total * factor + jnp.sum(weights, axis=0, keepdims=True)
        mixed = lax.dot_general(
            held[at, HD:],
            weights.astype(BF16),
            (((0,), (0,)), ((), ())),
            preferred_element_type=F32,
        )
        return new_top, total, acc * factor + mixed

    state = (
        jnp.full((1, group_size * rows), -1e30, F32),
        jnp.zeros((1, group_size * rows), F32),
        jnp.zeros((HD, group_size * rows), F32),
    )
    state = block(own, 1, state, masked=True)
    pairs = own // 2
    state = lax.fori_loop(0, pairs, lambda j, held_state: block(2 * j, 2, held_state), state)
    state = lax.fori_loop(2 * pairs, own, lambda j, held_state: block(j, 1, held_state), state)
    _, total, acc = state
    acc = acc / total
    for g in range(group_size):
        out_ref[:, g * HD : (g + 1) * HD] = acc[:, g * rows : (g + 1) * rows].T.astype(BF16)


def attend(own, queries, pieces, places):
    rows, width = queries.shape
    count = sum(p.shape[0] for p in pieces)
    whole = pl.BlockSpec((rows, width), lambda g, s: (0, 0))
    return pl.pallas_call(
        functools.partial(attend_kernel, group_size=width // HD),
        out_shape=jax.ShapeDtypeStruct((rows, width), BF16),
        grid_spec=pltpu.PrefetchScalarGridSpec(
            num_scalar_prefetch=1,
            grid=(1,),
            in_specs=[whole] + [pl.BlockSpec(p.shape, lambda g, s: (0, 0)) for p in pieces],
            out_specs=whole,
            scratch_shapes=[pltpu.VMEM((count, 2 * HD), BF16)],
        ),
        compiler_params=pltpu.CompilerParams(vmem_limit_bytes=VMEM_LIMIT),
        cost_estimate=pl.CostEstimate(
            flops=4 * rows * count * width,
            bytes_accessed=4 * count * HD,
            transcendentals=rows * count * width // HD,
        ),
        name="attend",
    )(jnp.stack([own] + places).astype(jnp.int32), queries, *pieces)


def hidden_tile(hidden):
    return 256 if hidden % 256 == 0 else 128


def scale_share(code_ref, shares, gain_ref, router_ref, scaled_ref):
    value = choose(code_ref[1], shares).astype(F32)
    scaled = (value * gain_ref[...].astype(F32)).astype(BF16)
    scaled_ref[...] = scaled

    def lanes(wide):
        return sum(wide[:, at : at + 128] for at in range(0, wide.shape[1], 128))

    return lanes(value * value), lanes(scaled.astype(F32) * router_ref[...].astype(F32))


def share_kernel(code_ref, *refs, shares, added):
    gain_ref, router_ref, gate_ref, up_ref = refs[shares : shares + 4]
    totals, outs, scaled = refs[shares + 4 : -5], refs[-5:-1], refs[-1]

    @pl.when(pl.program_id(0) == 0)
    def _():
        parts = scale_share(code_ref, refs[:shares], gain_ref, router_ref, scaled)
        for number, part in enumerate(parts):
            outs[2 + number][...] = part + totals[2 + number][...] if added else part

    for number, mat in enumerate((gate_ref, up_ref)):
        part = dot32(scaled[...], mat[0])
        outs[number][...] = part + totals[number][...] if added else part


def expert_share(code, shares, gains, router_row, w_gate, w_up, totals, which):
    rows, width = shares[0].shape
    hidden = w_gate.shape[2]
    tile = hidden_tile(hidden)
    sums = [pl.BlockSpec((rows, tile), lambda t, s: (0, t))] * 2 + [
        pl.BlockSpec((rows, 128), lambda t, s: (0, 0))
    ] * 2
    return pl.pallas_call(
        functools.partial(share_kernel, shares=len(shares), added=totals is not None),
        out_shape=[jax.ShapeDtypeStruct((rows, n), F32) for n in (hidden, hidden, 128, 128)],
        grid_spec=pltpu.PrefetchScalarGridSpec(
            num_scalar_prefetch=1,
            grid=(hidden // tile,),
            in_specs=[pl.BlockSpec((rows, width), lambda t, s: (0, 0))] * len(shares)
            + [pl.BlockSpec((1, width), lambda t, s: (0, s[0]))] * 2
            + [pl.BlockSpec((1, width, tile), lambda t, s: (which, s[0], t))] * 2
            + (sums if totals is not None else []),
            out_specs=sums,
            scratch_shapes=[pltpu.VMEM((rows, width), BF16)],
        ),
        compiler_params=pltpu.CompilerParams(vmem_limit_bytes=VMEM_LIMIT),
        cost_estimate=SMALL,
        name="expert_share",
    )(code, *shares, gains, router_row, w_gate, w_up, *(totals or ()))


def finish_kernel(code_ref, *refs, shares, tiles, full_width):
    gain_ref, router_ref, gate_ref, up_ref = refs[shares : shares + 4]
    gate_sum, up_sum, squares_sum, logits_sum, down_ref, out_ref = refs[shares + 4 : shares + 10]
    scaled, factor, hidden = refs[-3:]
    step = pl.program_id(0)

    @pl.when(step == 0)
    def _():
        squares, logits = scale_share(code_ref, refs[:shares], gain_ref, router_ref, scaled)
        squares = jnp.sum(squares + squares_sum[...], axis=-1, keepdims=True)
        logit = jnp.sum(logits + logits_sum[...], axis=-1, keepdims=True)
        inverse = lax.rsqrt(squares / full_width + epsilon)
        score = 1.0 / (1.0 + jnp.exp(-logit * inverse))
        factor[...] = jnp.broadcast_to(inverse * score, factor.shape)

    @pl.when(step < tiles)
    def _():
        scale = factor[:, :1]
        gate = (dot32(scaled[...], gate_ref[0]) + gate_sum[...]) * scale
        up = (dot32(scaled[...], up_ref[0]) + up_sum[...]) * scale
        hidden[step] = (gate / (1.0 + jnp.exp(-gate)) * up).astype(BF16)

    @pl.when(step >= tiles)
    def _():
        tile = hidden.shape[2]
        total = None
        for t in range(tiles):
            part = dot32(hidden[t], down_ref[0, t * tile : (t + 1) * tile, :])
            total = part if total is None else total + part
        out_ref[0] = total.astype(BF16)


def expert_finish(code, shares, gains, router_row, w_gate, w_up, totals, w_down, which):
    rows, width = shares[0].shape
    hidden = w_gate.shape[2]
    count = w_down.shape[2] // width
    tile = hidden_tile(hidden)
    tiles = hidden // tile

    def at(t):
        return jnp.minimum(t, tiles - 1)

    def after_tiles(t):
        return jnp.maximum(t - tiles, 0)

    return pl.pallas_call(
        functools.partial(
            finish_kernel, shares=len(shares), tiles=tiles, full_width=w_down.shape[2]
        ),
        out_shape=jax.ShapeDtypeStruct((count, rows, width), BF16),
        grid_spec=pltpu.PrefetchScalarGridSpec(
            num_scalar_prefetch=1,
            grid=(tiles + count,),
            in_specs=[pl.BlockSpec((rows, width), lambda t, s: (0, 0))] * len(shares)
            + [pl.BlockSpec((1, width), lambda t, s: (0, s[0]))] * 2
            + [pl.BlockSpec((1, width, tile), lambda t, s: (which, s[0], at(t)))] * 2
            + [pl.BlockSpec((rows, tile), lambda t, s: (0, at(t)))] * 2
            + [pl.BlockSpec((rows, 128), lambda t, s: (0, 0))] * 2
            + [
                pl.BlockSpec(
                    (1, hidden, width),
                    lambda t, s: (which, 0, lax.rem(s[2] + after_tiles(t), count)),
                )
            ],
            out_specs=pl.BlockSpec((1, rows, width), lambda t, s: (after_tiles(t), 0, 0)),
            scratch_shapes=[
                pltpu.VMEM((rows, width), BF16),
                pltpu.VMEM((rows, 128), F32),
                pltpu.VMEM((tiles, rows, tile), BF16),
            ],
        ),
        compiler_params=pltpu.CompilerParams(vmem_limit_bytes=VMEM_LIMIT),
        cost_estimate=SMALL,
        name="expert_finish",
    )(code, *shares, gains, router_row, w_gate, w_up, *totals, w_down)


def attention_share(tokens, own_tokens, attn_gain, w_query, w_key, w_value, w_out):
    ctx_index = lax.axis_index("ctx")
    kv_heads = w_key.shape[1] // HD
    group_width = w_query.shape[1] // kv_heads
    normed = root_norm(tokens, attn_gain)
    queries, keys, values = (
        dot32(normed, lax.all_gather(w, "ctx", axis=0, tiled=True)).astype(BF16)
        for w in (w_query, w_key, w_value)
    )
    keys = lax.all_gather(keys, "ctx", axis=0, tiled=True)
    values = lax.all_gather(values, "ctx", axis=0, tiled=True)
    places = [jnp.int32(b) for b in range(lax.axis_size("ctx"))]
    attended = []
    for g in range(kv_heads):
        head = slice(g * HD, (g + 1) * HD)
        piece = jnp.concatenate([keys[:, head], values[:, head]], axis=1)
        query = queries[:, g * group_width : (g + 1) * group_width]
        attended.append(attend(ctx_index, query, [piece], places))
    partial = dot32(jnp.concatenate(attended, axis=1), w_out).astype(BF16)
    attn_sum = lax.psum_scatter(partial, "hx", scatter_dimension=1, tiled=True)
    return (own_tokens.astype(F32) + attn_sum.astype(F32)).astype(BF16)


def paired_attention_share(tokens, own_tokens, attn_gain, w_query, w_key, w_value, w_out):
    ctx_count = lax.axis_size("ctx")
    hx_count = lax.axis_size("hx")
    ctx_index = lax.axis_index("ctx")
    hx_index = lax.axis_index("hx")
    parity = ctx_index % 2
    tok_rows, full_width = tokens.shape
    width = full_width // hx_count
    kv_heads = w_key.shape[1] // HD // 2
    kv_width = kv_heads * HD
    query_width = w_query.shape[1] // 2
    group_width = query_width // kv_heads

    def side(matrix, which, size, axis=1):
        return lax.dynamic_slice_in_dim(matrix, which * size, size, axis)

    own_kv = jnp.concatenate([side(m, parity, kv_width) for m in (w_key, w_value)], axis=1)
    own_query = side(w_query, parity, query_width)
    other_kv = jnp.concatenate([side(m, 1 - parity, kv_width) for m in (w_key, w_value)], axis=1)
    take = swap(other_kv, "ctx", 1)
    take_query = swap(side(w_query, after(1 - parity, take), query_width), "ctx", 1)
    other_tokens = swap(after(tokens, take_query), "ctx", 1)
    middle = hx_count // 2 if hx_count > 2 else 0
    half_rows = query_width // 2
    moves = []
    for k in [k for k in range(1, hx_count) if k != middle] + [middle] * (middle > 0):
        pieces = ((0, half_rows), (half_rows, half_rows)) if k == middle else ((0, query_width),)
        moves += [(k, *piece) for piece in pieces]

    def out_block(k, first_row, size, row_at):
        place = (row_at + first_row, (hx_index + k) % hx_count * width)
        return lax.dynamic_slice(w_out, place, (size, width))

    out_parts = {}

    def next_block(*earlier):
        if not moves:
            return None
        k, first_row, size = moves.pop(0)
        return k, out_block(k, first_row, size, after(parity * query_width, *earlier))

    def move(sent, *earlier):
        if sent is None:
            return ()
        k, block = sent
        block = after(block, *earlier) if earlier else block
        out_parts.setdefault(k, []).append(ring_shift(block, k))
        return (out_parts[k][-1],)

    def ready(sent):
        return () if sent is None else (sent[1],)

    def in_order(own, other):
        pair = (jnp.where(parity == 0, own, other), jnp.where(parity == 0, other, own))
        return jnp.concatenate(pair, axis=0)

    kv_mats = in_order(own_kv, take)
    query_mats = in_order(own_query, take_query)

    def together(arrived, *others):
        flat, tree = jax.tree.flatten(arrived)
        flat = lax.optimization_barrier(tuple(flat) + others)
        return jax.tree.unflatten(tree, flat[: len(flat) - len(others)])

    def pair_at(offset):
        return (ctx_index ^ offset) // 2

    def project_near(mats, near):
        places = [pair_at(0), pair_at(2), pair_at(4)]
        return project(normed, [mats, near[2], near[4]], places, None, F32)

    def project_far(far, total):
        places = [2 * pair_at(6), 2 * pair_at(6) + 1]
        return project(normed, list(far), places, total, BF16)

    normed = [norm_rows(t, attn_gain) for t in (tokens, other_tokens)]
    sent = next_block(take)
    following = next_block(take_query)
    kv_near = together(
        near_blocks(kv_mats), *move(sent), *ready(following), other_tokens, normed[0], own_tokens
    )
    first = kv_near[2]
    sent, following = following, next_block(first)
    kv_total = project_near(kv_mats, kv_near)
    kv_far, query_near, kv_total = together(
        (far_block(kv_near), near_blocks(after(query_mats, first)), kv_total),
        *move(sent, first),
        *ready(following),
    )
    before, first = first, query_near[2]
    sent, following = following, next_block(before)
    kv_pair = jnp.concatenate(project_far(kv_far, kv_total), axis=0)
    query_total = project_near(query_mats, query_near)
    block_near, query_far, query_total = together(
        (near_blocks(kv_pair), far_block(query_near), query_total),
        *move(sent, first),
        *ready(following),
    )
    first = block_near[2]
    last_move = move(following, first)
    out_parts[0] = [out_block(0, 0, query_width, after(parity * query_width, first))]
    block_far = far_block(block_near)
    queries = project_far(query_far, query_total)
    pieces = [kv_pair, block_near[2], block_near[4], *block_far]
    places = [ctx_index ^ o ^ j for o in (0, 2, 4, 6) for j in (0, 1)]

    def head(piece, g):
        if kv_heads == 1:
            return piece
        columns = [piece[:, h * HD : (h + 1) * HD] for h in (g, kv_heads + g)]
        return jnp.concatenate(columns, axis=1)

    lefts = {}
    for j in (1, 0):
        attended = [
            attend(
                ctx_index ^ j,
                queries[j][:, g * group_width : (g + 1) * group_width],
                [head(piece, g) for piece in pieces],
                places,
            )
            for g in range(kv_heads)
        ]
        attended = jnp.concatenate(attended, axis=1)
        if j == 1:
            attended = after(attended, *last_move) if last_move else attended
        lefts[j] = [attended] + [x for pair in line_gather(attended) for x in pair]
    flat = lax.optimization_barrier(tuple(lefts[1]) + tuple(lefts[0]))
    lefts = {1: flat[: len(lefts[1])], 0: flat[len(lefts[1]) :]}
    table = np.zeros((hx_count, hx_count), np.int32)
    for own, entries in enumerate(arrival_order(hx_count)):
        for source, number in entries:
            table[own, (own - source) % hx_count] = 1 + number
    used = sorted(set(table.reshape(-1).tolist()))
    table = np.searchsorted(used, table).astype(np.int32)
    lefts = {j: [lefts[j][number] for number in used] for j in lefts}
    numbers = tuple(tuple(sorted(set(table[:, k].tolist()))) for k in range(hx_count))
    codes = jnp.asarray(table)[hx_index]
    rights = [out_parts[k] for k in range(hx_count)]
    given = swap(sum_dots(codes, numbers, lefts[1], rights, ()), "ctx", 1)
    return sum_dots(codes, numbers, lefts[0], rights, (given, own_tokens))


def body(
    tokens,
    attn_gain,
    ffn_gain,
    w_query,
    w_key,
    w_value,
    w_out,
    w_router,
    routes,
    w_gate,
    w_up,
    w_down,
):
    ctx_count = lax.axis_size("ctx")
    hx_count = lax.axis_size("hx")
    ctx_index = lax.axis_index("ctx")
    hx_index = lax.axis_index("hx")
    tok_rows, full_width = tokens.shape
    width = full_width // hx_count
    expert_count = w_router.shape[1]

    chosen = routes[:, 0]
    onehot = chosen[:, None] == jnp.arange(expert_count, dtype=jnp.int32)[None, :]
    counts = jnp.cumsum(onehot.astype(jnp.int32), axis=0)
    position = jnp.sum(jnp.where(onehot, counts, 0), axis=-1) - 1
    capacity = tok_rows // 8
    part = capacity // CHUNKS
    exp_local = w_gate.shape[0]
    slot_expert = jnp.arange(expert_count * part, dtype=jnp.int32) // part
    slot_place = jnp.arange(expert_count * part, dtype=jnp.int32) % part
    pickers = [
        (
            (slot_expert[:, None] == chosen[None, :])
            & (slot_place[:, None] + c * part == position[None, :])
        ).astype(BF16)
        for c in range(CHUNKS)
    ]

    paired = ctx_count // 2 == 4 and (w_key.shape[1] // HD) % 2 == 0
    share_of = paired_attention_share if paired else attention_share
    own_tokens = lax.dynamic_slice_in_dim(tokens, hx_index * width, width, 1)
    stream = share_of(tokens, own_tokens, attn_gain, w_query, w_key, w_value, w_out)

    gains = ffn_gain.reshape(1, full_width)
    router_rows = w_router.T
    order = arrival_order(hx_count)
    codes = [jnp.stack([hx_index, jnp.int32(0), hx_index]).astype(jnp.int32)]
    arrays = [None]
    for t in range(hx_count - 1):
        found = np.array([entries[t] for entries in order], np.int32)
        arrays.append(sorted(set(found[:, 1].tolist())))
        found[:, 1] = np.searchsorted(arrays[-1], found[:, 1])
        codes.append(jnp.concatenate([jnp.asarray(found)[hx_index], codes[0][2:]]))

    def give_back(c, reduced):
        reduced = jnp.stack([r.reshape(ctx_count, part, width) for r in reduced], axis=1)
        returned = lax.all_to_all(reduced, "ctx", split_axis=0, concat_axis=0, tiled=True)
        return returned.reshape(expert_count * part, width)

    rows = [slice(e * ctx_count * part, (e + 1) * ctx_count * part) for e in range(exp_local)]
    router = [
        lax.dynamic_slice_in_dim(router_rows, ctx_index * exp_local + e, 1, 0)
        for e in range(exp_local)
    ]

    def take_rows(c, *earlier):
        sent = dot32(pickers[c], stream).astype(BF16)
        sent = sent.reshape(ctx_count, exp_local, part, width)
        sent = after(sent, *earlier) if earlier else sent
        taken = lax.all_to_all(sent, "ctx", split_axis=0, concat_axis=0, tiled=True)
        taken = taken.reshape(ctx_count, exp_local, part, width)
        return taken.swapaxes(0, 1).reshape(exp_local * ctx_count * part, width)

    def add_shares(t, shares, totals):
        return [
            expert_share(
                codes[t], [x[rows[e]] for x in shares], gains, router[e], w_gate, w_up, totals[e], e
            )
            for e in range(exp_local)
        ]

    def held_back(values, totals):
        marks = tuple(x for sums in totals for x in sums[2:])
        return lax.optimization_barrier(tuple(values) + marks)[: len(values)]

    def after_all(values, earlier):
        return lax.optimization_barrier(tuple(values) + tuple(earlier))[: len(values)]

    none = [None] * exp_local
    returned = []
    scatter, arrived = None, ()
    taken = take_rows(0)
    totals = None
    for c in range(CHUNKS):
        gather = line_gather(taken)
        following = None
        shares = []
        for t in range(hx_count - 1):
            inner = 0 < t < hx_count - 2
            if inner and scatter:
                totals = add_shares(t, [shares[n] for n in arrays[t]], totals)
            earlier = list(arrived) if t == hx_count - 2 else []
            if inner:
                earlier = [x for sums in totals for x in sums[2:]]
            elif t > 0 and following is not None:
                earlier.append(following)
            pair = next(gather) if t == 0 else gather.send(earlier)
            if t == 0:
                totals = totals or add_shares(0, [taken], none)
            elif not (inner and scatter):
                if inner:
                    shares = list(after_all(shares, pair))
                totals = add_shares(t, [shares[n] for n in arrays[t]], totals)
            if t == 0 and c + 1 < CHUNKS:
                following = take_rows(c + 1, *pair)
            if scatter and t == hx_count - 2:
                arrived = [x for sums in scatter for x in next(sums)]
                pair = lax.optimization_barrier(tuple(pair) + tuple(arrived))[:2]
            shares = shares + list(pair)
        following_totals = None
        if c + 1 < CHUNKS:
            following_totals = add_shares(0, [following], none)
            taken = after(following, *shares[-2:])
            shares = held_back(shares, following_totals)
        outs = [
            expert_finish(
                codes[-1],
                [shares[n][rows[e]] for n in arrays[-1]],
                gains,
                router[e],
                w_gate,
                w_up,
                totals[e],
                w_down,
                e,
            )
            for e in range(exp_local)
        ]
        reduced = None
        if scatter:
            for _ in range(hx_count - 4):
                [next(sums) for sums in scatter]
            marks = [x for sums in totals for x in sums[2:]]
            reduced = [sums.send(marks) for sums in scatter]
            outs = [after(o, *reduced) for o in outs]
        totals = following_totals
        scatter = [line_scatter(o) for o in outs]
        arrived = [x for sums in scatter for x in next(sums)]
        if reduced:
            returned.append(give_back(c - 1, [after(r, *arrived) for r in reduced]))
    for step in range(hx_count - 3):
        [next(sums) for sums in scatter]
    reduced = [sums.send(returned) if hx_count > 2 else next(sums) for sums in scatter]
    returned.append(give_back(CHUNKS - 1, reduced))
    expert_out = sum(
        lax.dot_general(p, r, (((0,), (0,)), ((), ())), preferred_element_type=F32)
        for p, r in zip(pickers, returned)
    )
    return (stream.astype(F32) + expert_out).astype(BF16)


def solution(mesh):
    return jax.shard_map(
        body,
        mesh=mesh,
        in_specs=(
            P("ctx", None),
            P(),
            P(),
            P("ctx", "hx"),
            P("ctx", "hx"),
            P("ctx", "hx"),
            P("hx", None),
            P(),
            P("ctx", None),
            P("ctx", None, "hx"),
            P("ctx", None, "hx"),
            P("ctx", "hx", None),
        ),
        out_specs=P("ctx", "hx"),
        check_vma=False,
    )
```

```python
import functools

import jax
import jax.numpy as jnp
import numpy as np
from jax import lax
from jax.experimental import pallas as pl
from jax.experimental.pallas import tpu as pltpu
from jax.sharding import PartitionSpec as P

HD = 128
epsilon = 1e-05
LOG2E = 1.4426950408889634
CHUNKS = 2
F32 = jnp.float32
BF16 = jnp.bfloat16


def dot32(left, right):
    return jnp.dot(left, right, preferred_element_type=F32)


def root_norm(values, gains):
    floats = values.astype(F32)
    inverse = lax.rsqrt(jnp.mean(floats * floats, axis=-1, keepdims=True) + epsilon)
    return (floats * inverse * gains.astype(F32)).astype(BF16)


def swap(value, axis, offset):
    count = lax.axis_size(axis)
    return lax.ppermute(value, axis, [(i, i ^ offset) for i in range(count)])


def near_blocks(block):
    return {offset: swap(block, "ctx", offset) for offset in (2, 4)}


def far_block(near):
    half = near[2].shape[0] // 2
    return swap(near[4][:half], "ctx", 2), swap(near[2][half:], "ctx", 4)


def after(value, *earlier):
    return lax.optimization_barrier((value,) + earlier)[0]


def ring_shift(values, k):
    count = lax.axis_size("hx")
    return lax.ppermute(values, "hx", [(j, (j + k) % count) for j in range(count)])


def line_pairs(step, spread):
    count = lax.axis_size("hx")
    pairs = [[], []]
    for j in range(count - 1):
        if (j >= step - 1) if spread else (j < step):
            pairs[j % 2].append((j, j + 1))
        if (j + 1 <= count - step) if spread else (j + 1 >= count - step):
            pairs[j % 2].append((j + 1, j))
    return pairs


def pass_on(values, pairs):
    return lax.ppermute(values, "hx", pairs) if pairs else jnp.zeros_like(values)


def line_gather(block):
    count = lax.axis_size("hx")
    even_in = odd_in = block
    earlier = ()
    for step in range(1, count):
        pairs = line_pairs(step, True)
        if earlier:
            even_in, odd_in = lax.optimization_barrier((even_in, odd_in) + tuple(earlier))[:2]
        even_in, odd_in = (
            pass_on(odd_in, pairs[0]) if pairs[0] else None,
            pass_on(even_in, pairs[1]) if pairs[1] else None,
        )
        even_in = odd_in if even_in is None else even_in
        odd_in = even_in if odd_in is None else odd_in
        even_in, odd_in = lax.optimization_barrier((even_in, odd_in))
        earlier = yield (even_in, odd_in)


def arrival_order(count):
    table = []
    for own in range(count):
        entries = []
        for step in range(1, count):
            for source, swap_is_odd in (
                (own - step, own % 2 == 0),
                (own + step, own % 2 == 1),
            ):
                if 0 <= source < count:
                    entries.append((source, 2 * (step - 1) + swap_is_odd))
        table.append(entries)
    return table


def line_scatter(values):
    count = lax.axis_size("hx")
    odd = lax.axis_index("hx") % 2 == 1
    even_in = odd_in = None
    for step in range(1, count):
        pairs = line_pairs(step, False)
        right, left = values[(count - step) % count], values[step % count]
        even_out, odd_out = jnp.where(odd, left, right), jnp.where(odd, right, left)
        if step > 1:
            even_out = (even_out.astype(F32) + odd_in.astype(F32)).astype(BF16)
            odd_out = (odd_out.astype(F32) + even_in.astype(F32)).astype(BF16)
            earlier = tuple(earlier or ())
            even_out, odd_out = lax.optimization_barrier((even_out, odd_out) + earlier)[:2]
        even_in, odd_in = pass_on(even_out, pairs[0]), pass_on(odd_out, pairs[1])
        if step < count - 1:
            earlier = yield (even_in, odd_in)
    total = values[0].astype(F32)
    if count > 1:
        total = total + even_in.astype(F32) + odd_in.astype(F32)
    yield total.astype(BF16)


SMALL = pl.CostEstimate(flops=0, bytes_accessed=4096, transcendentals=0)
VMEM_LIMIT = 48 * 1024 * 1024


def norm_kernel(values_ref, gains_ref, out_ref):
    floats = values_ref[...].astype(F32)
    inverse = lax.rsqrt(jnp.mean(floats * floats, axis=-1, keepdims=True) + epsilon)
    out_ref[...] = (floats * inverse * gains_ref[...].astype(F32)).astype(BF16)


def norm_rows(values, gains):
    rows, columns = values.shape
    tile = min(rows, 128)
    return pl.pallas_call(
        norm_kernel,
        out_shape=jax.ShapeDtypeStruct((rows, columns), BF16),
        grid=(rows // tile,),
        in_specs=[
            pl.BlockSpec((tile, columns), lambda r: (r, 0)),
            pl.BlockSpec((1, columns), lambda r: (0, 0)),
        ],
        out_specs=pl.BlockSpec((tile, columns), lambda r: (r, 0)),
        compiler_params=pltpu.CompilerParams(vmem_limit_bytes=VMEM_LIMIT),
        cost_estimate=SMALL,
        name="norm_rows",
    )(values, gains.reshape(1, columns))


def choose(code, refs, numbers=None):
    first, *others = numbers or range(len(refs))
    value = refs[first][...]
    for number in others:
        value = jnp.where(code == number, refs[number][...], value)
    return value


def sum_dots_kernel(codes_ref, *refs, lefts, splits, added, numbers):
    left, right, chosen = refs[:lefts], refs[lefts : lefts + sum(splits)], refs[-1]
    out_ref = refs[-2]

    @pl.when(pl.program_id(0) == 0)
    def _():
        for k in range(len(splits)):
            chosen[k] = choose(codes_ref[k], left, numbers[k])

    total = None
    for more in refs[lefts + sum(splits) : lefts + sum(splits) + added]:
        part = more[...].astype(F32)
        total = part if total is None else total + part
    number = 0
    for k, split in enumerate(splits):
        at = 0
        for _ in range(split):
            rows = right[number].shape[0]
            part = dot32(chosen[k, :, at : at + rows], right[number][...])
            total = part if total is None else total + part
            at += rows
            number += 1
    out_ref[...] = total.astype(out_ref.dtype)


def sum_dots(codes, numbers, lefts, rights, added):
    rows, columns = lefts[0].shape[0], rights[0][0].shape[1]
    tile = 256 if columns % 256 == 0 else 128
    flat = [m for mats in rights for m in mats]
    out = pl.BlockSpec((rows, tile), lambda c, s: (0, c))
    return pl.pallas_call(
        functools.partial(
            sum_dots_kernel,
            lefts=len(lefts),
            splits=tuple(len(mats) for mats in rights),
            added=len(added),
            numbers=numbers,
        ),
        out_shape=jax.ShapeDtypeStruct((rows, columns), BF16),
        grid_spec=pltpu.PrefetchScalarGridSpec(
            num_scalar_prefetch=1,
            grid=(columns // tile,),
            in_specs=[pl.BlockSpec(m.shape, lambda c, s: (0, 0)) for m in lefts]
            + [pl.BlockSpec((m.shape[0], tile), lambda c, s: (0, c)) for m in flat]
            + [out] * len(added),
            out_specs=out,
            scratch_shapes=[pltpu.VMEM((len(rights),) + lefts[0].shape, BF16)],
        ),
        compiler_params=pltpu.CompilerParams(vmem_limit_bytes=VMEM_LIMIT),
        cost_estimate=SMALL,
        name="sum_dots",
    )(codes, *lefts, *flat, *added)


def project_kernel(places_ref, *refs, count, mats, added):
    del places_ref
    outs = refs[len(refs) - count :]
    for j in range(count):
        total = refs[(count + 1) * mats + j][...] if added else None
        for k in range(mats):
            part = dot32(refs[j * mats + k][...], refs[count * mats + k][...])
            total = part if total is None else total + part
        outs[j][...] = total.astype(outs[j].dtype)


def project(values, mats, places, totals, dtype):
    rows = values[0].shape[0]
    columns = mats[0].shape[1]
    whole = pl.BlockSpec((rows, columns), lambda g, s: (0, 0))

    def columns_at(k):
        return pl.BlockSpec((rows, mats[k].shape[0]), lambda g, s: (0, s[k]))

    return pl.pallas_call(
        functools.partial(
            project_kernel, count=len(values), mats=len(mats), added=totals is not None
        ),
        out_shape=[jax.ShapeDtypeStruct((rows, columns), dtype) for _ in values],
        grid_spec=pltpu.PrefetchScalarGridSpec(
            num_scalar_prefetch=1,
            grid=(1,),
            in_specs=[columns_at(k) for _ in values for k in range(len(mats))]
            + [pl.BlockSpec(m.shape, lambda g, s: (0, 0)) for m in mats]
            + [whole] * len(totals or ()),
            out_specs=[whole] * len(values),
        ),
        compiler_params=pltpu.CompilerParams(vmem_limit_bytes=VMEM_LIMIT),
        cost_estimate=SMALL,
        name="project",
    )(
        jnp.stack(places).astype(jnp.int32),
        *[v for v in values for _ in mats],
        *mats,
        *(totals or ()),
    )


def attend_kernel(places_ref, query_ref, *refs, group_size):
    *pieces, out_ref, held = refs
    rows = query_ref.shape[0]
    own = places_ref[0]
    scale = HD ** (-0.5) * LOG2E
    queries = jnp.concatenate(
        [query_ref[:, g * HD : (g + 1) * HD] for g in range(group_size)], axis=0
    )

    number = 1
    for piece in pieces:
        for start in range(0, piece.shape[0], rows):
            to = pl.multiple_of(places_ref[number] * rows, rows)
            held[pl.ds(to, rows), :] = piece[start : start + rows, :]
            number += 1

    def block(first, count, state, masked=False):
        at = pl.ds(pl.multiple_of(first * rows, rows), count * rows)
        top, total, acc = state
        scores = lax.dot_general(
            held[at, :HD], queries, (((1,), (1,)), ((), ())), preferred_element_type=F32
        )
        if masked:
            key_at = lax.broadcasted_iota(jnp.int32, scores.shape, 0)
            query_at = lax.broadcasted_iota(jnp.int32, scores.shape, 1) % rows
            scores = jnp.where(key_at <= query_at, scores, -1e30)
        new_top = jnp.maximum(top, jnp.max(scores, axis=0, keepdims=True))
        weights = jnp.exp2((scores - new_top) * scale)
        factor = jnp.exp2((top - new_top) * scale)
        total = total * factor + jnp.sum(weights, axis=0, keepdims=True)
        mixed = lax.dot_general(
            held[at, HD:],
            weights.astype(BF16),
            (((0,), (0,)), ((), ())),
            preferred_element_type=F32,
        )
        return new_top, total, acc * factor + mixed

    state = (
        jnp.full((1, group_size * rows), -1e30, F32),
        jnp.zeros((1, group_size * rows), F32),
        jnp.zeros((HD, group_size * rows), F32),
    )
    state = block(own, 1, state, masked=True)
    pairs = own // 2
    state = lax.fori_loop(0, pairs, lambda j, held_state: block(2 * j, 2, held_state), state)
    state = lax.fori_loop(2 * pairs, own, lambda j, held_state: block(j, 1, held_state), state)
    _, total, acc = state
    acc = acc / total
    for g in range(group_size):
        out_ref[:, g * HD : (g + 1) * HD] = acc[:, g * rows : (g + 1) * rows].T.astype(BF16)


def attend(own, queries, pieces, places):
    rows, width = queries.shape
    count = sum(p.shape[0] for p in pieces)
    whole = pl.BlockSpec((rows, width), lambda g, s: (0, 0))
    return pl.pallas_call(
        functools.partial(attend_kernel, group_size=width // HD),
        out_shape=jax.ShapeDtypeStruct((rows, width), BF16),
        grid_spec=pltpu.PrefetchScalarGridSpec(
            num_scalar_prefetch=1,
            grid=(1,),
            in_specs=[whole] + [pl.BlockSpec(p.shape, lambda g, s: (0, 0)) for p in pieces],
            out_specs=whole,
            scratch_shapes=[pltpu.VMEM((count, 2 * HD), BF16)],
        ),
        compiler_params=pltpu.CompilerParams(vmem_limit_bytes=VMEM_LIMIT),
        cost_estimate=pl.CostEstimate(
            flops=4 * rows * count * width,
            bytes_accessed=4 * count * HD,
            transcendentals=rows * count * width // HD,
        ),
        name="attend",
    )(jnp.stack([own] + places).astype(jnp.int32), queries, *pieces)


def hidden_tile(hidden):
    return 256 if hidden % 256 == 0 else 128


def scale_share(code_ref, shares, gain_ref, router_ref, scaled_ref):
    value = choose(code_ref[1], shares).astype(F32)
    scaled = (value * gain_ref[...].astype(F32)).astype(BF16)
    scaled_ref[...] = scaled

    def lanes(wide):
        return sum(wide[:, at : at + 128] for at in range(0, wide.shape[1], 128))

    return lanes(value * value), lanes(scaled.astype(F32) * router_ref[...].astype(F32))


def share_kernel(code_ref, *refs, shares, added):
    gain_ref, router_ref, gate_ref, up_ref = refs[shares : shares + 4]
    totals, outs, scaled = refs[shares + 4 : -5], refs[-5:-1], refs[-1]

    @pl.when(pl.program_id(0) == 0)
    def _():
        parts = scale_share(code_ref, refs[:shares], gain_ref, router_ref, scaled)
        for number, part in enumerate(parts):
            outs[2 + number][...] = part + totals[2 + number][...] if added else part

    for number, mat in enumerate((gate_ref, up_ref)):
        part = dot32(scaled[...], mat[0])
        outs[number][...] = part + totals[number][...] if added else part


def expert_share(code, shares, gains, router_row, w_gate, w_up, totals, which):
    rows, width = shares[0].shape
    hidden = w_gate.shape[2]
    tile = hidden_tile(hidden)
    sums = [pl.BlockSpec((rows, tile), lambda t, s: (0, t))] * 2 + [
        pl.BlockSpec((rows, 128), lambda t, s: (0, 0))
    ] * 2
    return pl.pallas_call(
        functools.partial(share_kernel, shares=len(shares), added=totals is not None),
        out_shape=[jax.ShapeDtypeStruct((rows, n), F32) for n in (hidden, hidden, 128, 128)],
        grid_spec=pltpu.PrefetchScalarGridSpec(
            num_scalar_prefetch=1,
            grid=(hidden // tile,),
            in_specs=[pl.BlockSpec((rows, width), lambda t, s: (0, 0))] * len(shares)
            + [pl.BlockSpec((1, width), lambda t, s: (0, s[0]))] * 2
            + [pl.BlockSpec((1, width, tile), lambda t, s: (which, s[0], t))] * 2
            + (sums if totals is not None else []),
            out_specs=sums,
            scratch_shapes=[pltpu.VMEM((rows, width), BF16)],
        ),
        compiler_params=pltpu.CompilerParams(vmem_limit_bytes=VMEM_LIMIT),
        cost_estimate=SMALL,
        name="expert_share",
    )(code, *shares, gains, router_row, w_gate, w_up, *(totals or ()))


def finish_kernel(code_ref, *refs, shares, tiles, full_width):
    gain_ref, router_ref, gate_ref, up_ref = refs[shares : shares + 4]
    gate_sum, up_sum, squares_sum, logits_sum, down_ref, out_ref = refs[shares + 4 : shares + 10]
    scaled, factor, hidden = refs[-3:]
    step = pl.program_id(0)

    @pl.when(step == 0)
    def _():
        squares, logits = scale_share(code_ref, refs[:shares], gain_ref, router_ref, scaled)
        squares = jnp.sum(squares + squares_sum[...], axis=-1, keepdims=True)
        logit = jnp.sum(logits + logits_sum[...], axis=-1, keepdims=True)
        inverse = lax.rsqrt(squares / full_width + epsilon)
        score = 1.0 / (1.0 + jnp.exp(-logit * inverse))
        factor[...] = jnp.broadcast_to(inverse * score, factor.shape)

    @pl.when(step < tiles)
    def _():
        scale = factor[:, :1]
        gate = (dot32(scaled[...], gate_ref[0]) + gate_sum[...]) * scale
        up = (dot32(scaled[...], up_ref[0]) + up_sum[...]) * scale
        hidden[step] = (gate / (1.0 + jnp.exp(-gate)) * up).astype(BF16)

    @pl.when(step >= tiles)
    def _():
        tile = hidden.shape[2]
        total = None
        for t in range(tiles):
            part = dot32(hidden[t], down_ref[0, t * tile : (t + 1) * tile, :])
            total = part if total is None else total + part
        out_ref[0] = total.astype(BF16)


def expert_finish(code, shares, gains, router_row, w_gate, w_up, totals, w_down, which):
    rows, width = shares[0].shape
    hidden = w_gate.shape[2]
    count = w_down.shape[2] // width
    tile = hidden_tile(hidden)
    tiles = hidden // tile

    def at(t):
        return jnp.minimum(t, tiles - 1)

    def after_tiles(t):
        return jnp.maximum(t - tiles, 0)

    return pl.pallas_call(
        functools.partial(
            finish_kernel, shares=len(shares), tiles=tiles, full_width=w_down.shape[2]
        ),
        out_shape=jax.ShapeDtypeStruct((count, rows, width), BF16),
        grid_spec=pltpu.PrefetchScalarGridSpec(
            num_scalar_prefetch=1,
            grid=(tiles + count,),
            in_specs=[pl.BlockSpec((rows, width), lambda t, s: (0, 0))] * len(shares)
            + [pl.BlockSpec((1, width), lambda t, s: (0, s[0]))] * 2
            + [pl.BlockSpec((1, width, tile), lambda t, s: (which, s[0], at(t)))] * 2
            + [pl.BlockSpec((rows, tile), lambda t, s: (0, at(t)))] * 2
            + [pl.BlockSpec((rows, 128), lambda t, s: (0, 0))] * 2
            + [
                pl.BlockSpec(
                    (1, hidden, width),
                    lambda t, s: (which, 0, lax.rem(s[2] + after_tiles(t), count)),
                )
            ],
            out_specs=pl.BlockSpec((1, rows, width), lambda t, s: (after_tiles(t), 0, 0)),
            scratch_shapes=[
                pltpu.VMEM((rows, width), BF16),
                pltpu.VMEM((rows, 128), F32),
                pltpu.VMEM((tiles, rows, tile), BF16),
            ],
        ),
        compiler_params=pltpu.CompilerParams(vmem_limit_bytes=VMEM_LIMIT),
        cost_estimate=SMALL,
        name="expert_finish",
    )(code, *shares, gains, router_row, w_gate, w_up, *totals, w_down)


def attention_share(tokens, own_tokens, attn_gain, w_query, w_key, w_value, w_out):
    ctx_index = lax.axis_index("ctx")
    kv_heads = w_key.shape[1] // HD
    group_width = w_query.shape[1] // kv_heads
    normed = root_norm(tokens, attn_gain)
    queries, keys, values = (
        dot32(normed, lax.all_gather(w, "ctx", axis=0, tiled=True)).astype(BF16)
        for w in (w_query, w_key, w_value)
    )
    keys = lax.all_gather(keys, "ctx", axis=0, tiled=True)
    values = lax.all_gather(values, "ctx", axis=0, tiled=True)
    places = [jnp.int32(b) for b in range(lax.axis_size("ctx"))]
    attended = []
    for g in range(kv_heads):
        head = slice(g * HD, (g + 1) * HD)
        piece = jnp.concatenate([keys[:, head], values[:, head]], axis=1)
        query = queries[:, g * group_width : (g + 1) * group_width]
        attended.append(attend(ctx_index, query, [piece], places))
    partial = dot32(jnp.concatenate(attended, axis=1), w_out).astype(BF16)
    attn_sum = lax.psum_scatter(partial, "hx", scatter_dimension=1, tiled=True)
    return (own_tokens.astype(F32) + attn_sum.astype(F32)).astype(BF16)


def paired_attention_share(tokens, own_tokens, attn_gain, w_query, w_key, w_value, w_out):
    ctx_count = lax.axis_size("ctx")
    hx_count = lax.axis_size("hx")
    ctx_index = lax.axis_index("ctx")
    hx_index = lax.axis_index("hx")
    parity = ctx_index % 2
    tok_rows, full_width = tokens.shape
    width = full_width // hx_count
    kv_heads = w_key.shape[1] // HD // 2
    kv_width = kv_heads * HD
    query_width = w_query.shape[1] // 2
    group_width = query_width // kv_heads

    def side(matrix, which, size, axis=1):
        return lax.dynamic_slice_in_dim(matrix, which * size, size, axis)

    own_kv = jnp.concatenate([side(m, parity, kv_width) for m in (w_key, w_value)], axis=1)
    own_query = side(w_query, parity, query_width)
    other_kv = jnp.concatenate([side(m, 1 - parity, kv_width) for m in (w_key, w_value)], axis=1)
    take = swap(other_kv, "ctx", 1)
    take_query = swap(side(w_query, after(1 - parity, take), query_width), "ctx", 1)
    other_tokens = swap(after(tokens, take_query), "ctx", 1)
    middle = hx_count // 2 if hx_count > 2 else 0
    half_rows = query_width // 2
    moves = []
    for k in [k for k in range(1, hx_count) if k != middle] + [middle] * (middle > 0):
        pieces = ((0, half_rows), (half_rows, half_rows)) if k == middle else ((0, query_width),)
        moves += [(k, *piece) for piece in pieces]

    def out_block(k, first_row, size, row_at):
        place = (row_at + first_row, (hx_index + k) % hx_count * width)
        return lax.dynamic_slice(w_out, place, (size, width))

    out_parts = {}

    def next_block(*earlier):
        if not moves:
            return None
        k, first_row, size = moves.pop(0)
        return k, out_block(k, first_row, size, after(parity * query_width, *earlier))

    def move(sent, *earlier):
        if sent is None:
            return ()
        k, block = sent
        block = after(block, *earlier) if earlier else block
        out_parts.setdefault(k, []).append(ring_shift(block, k))
        return (out_parts[k][-1],)

    def ready(sent):
        return () if sent is None else (sent[1],)

    def in_order(own, other):
        pair = (jnp.where(parity == 0, own, other), jnp.where(parity == 0, other, own))
        return jnp.concatenate(pair, axis=0)

    kv_mats = in_order(own_kv, take)
    query_mats = in_order(own_query, take_query)

    def together(arrived, *others):
        flat, tree = jax.tree.flatten(arrived)
        flat = lax.optimization_barrier(tuple(flat) + others)
        return jax.tree.unflatten(tree, flat[: len(flat) - len(others)])

    def pair_at(offset):
        return (ctx_index ^ offset) // 2

    def project_near(mats, near):
        places = [pair_at(0), pair_at(2), pair_at(4)]
        return project(normed, [mats, near[2], near[4]], places, None, F32)

    def project_far(far, total):
        places = [2 * pair_at(6), 2 * pair_at(6) + 1]
        return project(normed, list(far), places, total, BF16)

    normed = [norm_rows(t, attn_gain) for t in (tokens, other_tokens)]
    sent = next_block(take)
    following = next_block(take_query)
    moved = move(sent)
    kv_near = together(
        near_blocks(kv_mats), *ready(following), other_tokens, normed[0], own_tokens
    )
    first = kv_near[2]
    sent, following = following, next_block(first)
    kv_total = project_near(kv_mats, kv_near)
    kv_far, query_near, kv_total = together(
        (far_block(kv_near), near_blocks(after(query_mats, first)), kv_total),
        *move(sent, first, *moved),
        *ready(following),
    )
    before, first = first, query_near[2]
    sent, following = following, next_block(before)
    kv_pair = jnp.concatenate(project_far(kv_far, kv_total), axis=0)
    query_total = project_near(query_mats, query_near)
    moved = move(sent, first)
    block_near, query_far, query_total = together(
        (near_blocks(kv_pair), far_block(query_near), query_total),
        *ready(following),
    )
    first = block_near[2]
    last_move = move(following, first, *moved)
    out_parts[0] = [out_block(0, 0, query_width, after(parity * query_width, first))]
    block_far = far_block(block_near)
    queries = project_far(query_far, query_total)
    pieces = [kv_pair, block_near[2], block_near[4], *block_far]
    places = [ctx_index ^ o ^ j for o in (0, 2, 4, 6) for j in (0, 1)]

    def head(piece, g):
        if kv_heads == 1:
            return piece
        columns = [piece[:, h * HD : (h + 1) * HD] for h in (g, kv_heads + g)]
        return jnp.concatenate(columns, axis=1)

    lefts = {}
    for j in (1, 0):
        attended = [
            attend(
                ctx_index ^ j,
                queries[j][:, g * group_width : (g + 1) * group_width],
                [head(piece, g) for piece in pieces],
                places,
            )
            for g in range(kv_heads)
        ]
        attended = jnp.concatenate(attended, axis=1)
        if j == 1:
            attended = after(attended, *last_move) if last_move else attended
        lefts[j] = [attended] + [x for pair in line_gather(attended) for x in pair]
    flat = lax.optimization_barrier(tuple(lefts[1]) + tuple(lefts[0]))
    lefts = {1: flat[: len(lefts[1])], 0: flat[len(lefts[1]) :]}
    table = np.zeros((hx_count, hx_count), np.int32)
    for own, entries in enumerate(arrival_order(hx_count)):
        for source, number in entries:
            table[own, (own - source) % hx_count] = 1 + number
    used = sorted(set(table.reshape(-1).tolist()))
    table = np.searchsorted(used, table).astype(np.int32)
    lefts = {j: [lefts[j][number] for number in used] for j in lefts}
    numbers = tuple(tuple(sorted(set(table[:, k].tolist()))) for k in range(hx_count))
    codes = jnp.asarray(table)[hx_index]
    rights = [out_parts[k] for k in range(hx_count)]
    given = swap(sum_dots(codes, numbers, lefts[1], rights, ()), "ctx", 1)
    return sum_dots(codes, numbers, lefts[0], rights, (given, own_tokens))


def body(
    tokens,
    attn_gain,
    ffn_gain,
    w_query,
    w_key,
    w_value,
    w_out,
    w_router,
    routes,
    w_gate,
    w_up,
    w_down,
):
    ctx_count = lax.axis_size("ctx")
    hx_count = lax.axis_size("hx")
    ctx_index = lax.axis_index("ctx")
    hx_index = lax.axis_index("hx")
    tok_rows, full_width = tokens.shape
    width = full_width // hx_count
    expert_count = w_router.shape[1]

    chosen = routes[:, 0]
    onehot = chosen[:, None] == jnp.arange(expert_count, dtype=jnp.int32)[None, :]
    counts = jnp.cumsum(onehot.astype(jnp.int32), axis=0)
    position = jnp.sum(jnp.where(onehot, counts, 0), axis=-1) - 1
    capacity = tok_rows // 8
    part = capacity // CHUNKS
    exp_local = w_gate.shape[0]
    slot_expert = jnp.arange(expert_count * part, dtype=jnp.int32) // part
    slot_place = jnp.arange(expert_count * part, dtype=jnp.int32) % part
    pickers = [
        (
            (slot_expert[:, None] == chosen[None, :])
            & (slot_place[:, None] + c * part == position[None, :])
        ).astype(BF16)
        for c in range(CHUNKS)
    ]

    paired = ctx_count // 2 == 4 and (w_key.shape[1] // HD) % 2 == 0
    share_of = paired_attention_share if paired else attention_share
    own_tokens = lax.dynamic_slice_in_dim(tokens, hx_index * width, width, 1)
    stream = share_of(tokens, own_tokens, attn_gain, w_query, w_key, w_value, w_out)

    gains = ffn_gain.reshape(1, full_width)
    router_rows = w_router.T
    order = arrival_order(hx_count)
    codes = [jnp.stack([hx_index, jnp.int32(0), hx_index]).astype(jnp.int32)]
    arrays = [None]
    for t in range(hx_count - 1):
        found = np.array([entries[t] for entries in order], np.int32)
        arrays.append(sorted(set(found[:, 1].tolist())))
        found[:, 1] = np.searchsorted(arrays[-1], found[:, 1])
        codes.append(jnp.concatenate([jnp.asarray(found)[hx_index], codes[0][2:]]))

    def give_back(c, reduced):
        reduced = jnp.stack([r.reshape(ctx_count, part, width) for r in reduced], axis=1)
        returned = lax.all_to_all(reduced, "ctx", split_axis=0, concat_axis=0, tiled=True)
        return returned.reshape(expert_count * part, width)

    rows = [slice(e * ctx_count * part, (e + 1) * ctx_count * part) for e in range(exp_local)]
    router = [
        lax.dynamic_slice_in_dim(router_rows, ctx_index * exp_local + e, 1, 0)
        for e in range(exp_local)
    ]

    def take_rows(c, *earlier):
        sent = dot32(pickers[c], stream).astype(BF16)
        sent = sent.reshape(ctx_count, exp_local, part, width)
        sent = after(sent, *earlier) if earlier else sent
        taken = lax.all_to_all(sent, "ctx", split_axis=0, concat_axis=0, tiled=True)
        taken = taken.reshape(ctx_count, exp_local, part, width)
        return taken.swapaxes(0, 1).reshape(exp_local * ctx_count * part, width)

    def add_shares(t, shares, totals):
        return [
            expert_share(
                codes[t], [x[rows[e]] for x in shares], gains, router[e], w_gate, w_up, totals[e], e
            )
            for e in range(exp_local)
        ]

    def held_back(values, totals):
        marks = tuple(x for sums in totals for x in sums[2:])
        return lax.optimization_barrier(tuple(values) + marks)[: len(values)]

    def after_all(values, earlier):
        return lax.optimization_barrier(tuple(values) + tuple(earlier))[: len(values)]

    none = [None] * exp_local
    returned = []
    scatter, arrived = None, ()
    taken = take_rows(0)
    totals = None
    for c in range(CHUNKS):
        gather = line_gather(taken)
        following = None
        shares = []
        for t in range(hx_count - 1):
            inner = 0 < t < hx_count - 2
            if inner and scatter:
                totals = add_shares(t, [shares[n] for n in arrays[t]], totals)
            earlier = list(arrived) if t == hx_count - 2 else []
            if inner:
                earlier = [x for sums in totals for x in sums[2:]]
            elif t > 0 and following is not None:
                earlier.append(following)
            pair = next(gather) if t == 0 else gather.send(earlier)
            if t == 0:
                totals = totals or add_shares(0, [taken], none)
            elif not (inner and scatter):
                if inner:
                    shares = list(after_all(shares, pair))
                totals = add_shares(t, [shares[n] for n in arrays[t]], totals)
            if t == 0 and c + 1 < CHUNKS:
                following = take_rows(c + 1, *pair)
            if scatter and t == hx_count - 2:
                arrived = [x for sums in scatter for x in next(sums)]
                pair = lax.optimization_barrier(tuple(pair) + tuple(arrived))[:2]
            shares = shares + list(pair)
        following_totals = None
        if c + 1 < CHUNKS:
            following_totals = add_shares(0, [following], none)
            taken = after(following, *shares[-2:])
            shares = held_back(shares, following_totals)
        outs = [
            expert_finish(
                codes[-1],
                [shares[n][rows[e]] for n in arrays[-1]],
                gains,
                router[e],
                w_gate,
                w_up,
                totals[e],
                w_down,
                e,
            )
            for e in range(exp_local)
        ]
        reduced = None
        if scatter:
            for _ in range(hx_count - 4):
                [next(sums) for sums in scatter]
            marks = [x for sums in totals for x in sums[2:]]
            reduced = [sums.send(marks) for sums in scatter]
            outs = [after(o, *reduced) for o in outs]
        totals = following_totals
        scatter = [line_scatter(o) for o in outs]
        arrived = [x for sums in scatter for x in next(sums)]
        if reduced:
            returned.append(give_back(c - 1, [after(r, *arrived) for r in reduced]))
    for step in range(hx_count - 3):
        [next(sums) for sums in scatter]
    reduced = [sums.send(returned) if hx_count > 2 else next(sums) for sums in scatter]
    returned.append(give_back(CHUNKS - 1, reduced))
    expert_out = sum(
        lax.dot_general(p, r, (((0,), (0,)), ((), ())), preferred_element_type=F32)
        for p, r in zip(pickers, returned)
    )
    return (stream.astype(F32) + expert_out).astype(BF16)


def solution(mesh):
    return jax.shard_map(
        body,
        mesh=mesh,
        in_specs=(
            P("ctx", None),
            P(),
            P(),
            P("ctx", "hx"),
            P("ctx", "hx"),
            P("ctx", "hx"),
            P("hx", None),
            P(),
            P("ctx", None),
            P("ctx", None, "hx"),
            P("ctx", None, "hx"),
            P("ctx", "hx", None),
        ),
        out_specs=P("ctx", "hx"),
        check_vma=False,
    )
```
